256 devices in a mesh: dp: 32 (over y, z), cam: 8 (over x, core).
Axes of the slice: x: 4, y: 4, z: 8, core: 2. Of those that a mesh axis runs over, the one named last changes fastest.
Arguments:
- x_in: bfloat16 [32, 8192, 1536], P('dp', 'cam'), may hold values from -6 to 6
- feat: bfloat16 [32, 8192, 1536], P('dp', 'cam'), may hold values from -6 to 6
- w_head: bfloat16 [1536, 192], replicated, may hold values from -0.15625 to 0.15625
- g_bev: bfloat16 [32, 32768, 128], P('dp', 'cam'), may hold values from -6 to 6
- cell_lists: int32 [32, 8, 8, 512], P('dp', 'cam'), may hold values from 0 to 4095, as said below
- point_slots: int32 [32, 8192, 64], P('dp', 'cam'), may hold values from 0 to 4096, as said below
- master: float32 [1536, 1728], P('dp'), may hold values from -0.15625 to 0.15625
- first_moment: float32 [1536, 1728], P('dp'), may hold values from -6 to 6
- second_moment: float32 [1536, 1728], P('dp'), may hold values from 0.5 to 4
Outputs:
- new_master: float32 [1536, 1728], P('dp')
- new_first: float32 [1536, 1728], P('dp')
- new_second: float32 [1536, 1728], P('dp')
The draws below stay inside these ranges and needn't reach their ends.
Inputs may be any that keep to these rules, and one draw needn't show every extreme that they name: `cell_lists`: each list of 512 cells that a pixel block asks of one tile is strictly increasing and holds cell numbers local to that tile. `point_slots`: an entry o * 512 + k names slot k of the list that the pixel's block asks of tile o; the entry 4096 marks a point outside the grid.
All inputs are finite; a program needn't handle non-finite values.
Results may differ from the reference program's by a relative error of at most 0.0006.
Values may be sent and summed in bfloat16 or wider, within the bound.
No kernel may reach another device: no remote copies, remote signals or barrier semaphores. Data moves between devices by JAX's collectives and lax.ppermute only.
A program may use at most 128 MiB of HBM per device.

```python
import math
import jax
import jax.numpy as jnp
from jax import lax

D = 1536
C = 128
DEPTH = 64
PIX = 1024
TILE = 4096
CAP = 512
HEAD = 192
SCENES = 32
PIXELS = 8192
N_CAM = 8


def draw_cell_lists(key, part):
    key = jax.random.fold_in(key, 11)
    list_total = SCENES * N_CAM * N_CAM
    list_keys = jax.random.split(key, list_total)

    def one_list(list_key):
        inner = jax.random.permutation(list_key, TILE - 2)[:CAP - 2].astype(jnp.int32) + 1
        full_list = jnp.concatenate([jnp.zeros((1,), jnp.int32), inner, jnp.full((1,), TILE - 1, jnp.int32)])
        return jnp.sort(full_list)
    return jax.vmap(one_list)(list_keys).reshape(SCENES, N_CAM, N_CAM, CAP).astype(jnp.int32)


def draw_point_slots(key, part):
    key = jax.random.fold_in(key, 23)
    key_near, key_far, key_pick, key_slot, key_out = jax.random.split(key, 5)
    dims_shape = (SCENES, N_CAM * PIX, DEPTH)
    requester = (jnp.arange(N_CAM * PIX, dtype=jnp.int32) // PIX)[None, :, None]
    nearby = requester + jax.random.randint(key_near, dims_shape, -1, 2)
    anywhere = jax.random.randint(key_far, dims_shape, 0, N_CAM)
    pick_far = jax.random.randint(key_pick, dims_shape, 0, 4) == 0
    owner_cam = jnp.mod(jnp.where(pick_far, anywhere, nearby), N_CAM)
    slot_index = jax.random.randint(key_slot, dims_shape, 0, CAP)
    outside = jax.random.randint(key_out, dims_shape, 0, 8) == 0
    slot_value = jnp.where(outside, N_CAM * CAP, owner_cam * CAP + slot_index)
    slot_value = slot_value.at[:, 0, 0].set(N_CAM * CAP).at[:, 0, 1].set(0)
    return slot_value.astype(jnp.int32)


def levels(rng, extent, cuts, least, top_value):
    factor_of = 1.0
    for dim, shards_of in cuts:
        steps = jax.random.uniform(jax.random.fold_in(jax.random.fold_in(rng, 6), dim), (shards_of,), jnp.float32, least / len(cuts), top_value / len(cuts))
        factor_of = factor_of * jnp.repeat(jnp.exp(steps), extent[dim] // shards_of).reshape((-1,) + (1,) * (len(extent) - 1 - dim))
    return factor_of


def noise(key, extent, scale, most, cuts=(), kind=jnp.bfloat16):
    gain = levels(key, extent, cuts, -0.22, 0.18) if cuts else 1.0
    array = jax.random.normal(key, extent, jnp.float32) * scale * gain
    return jnp.minimum(jnp.maximum(array, -most), most).astype(kind)


def setup_inputs(seed: int = 0) -> dict:
    keys = jax.random.split(jax.random.key(seed), 10)
    return {
        "x_in": noise(keys[0], (SCENES, PIXELS, D), 1.0, 6.0, ((0, 32), (1, 8))),
        "feat": noise(keys[1], (SCENES, PIXELS, D), 1.0, 6.0, ((0, 32), (1, 8))),
        "w_head": noise(keys[2], (D, HEAD), D ** -0.5, 0.15625),
        "g_bev": noise(keys[3], (SCENES, N_CAM * TILE, C), 1.0, 6.0, ((0, 32), (1, 8))),
        "cell_lists": draw_cell_lists(jax.random.fold_in(keys[9], 71), 0),
        "point_slots": draw_point_slots(jax.random.fold_in(keys[9], 71), 0),
        "master": noise(keys[6], (D, D + HEAD), D ** -0.5, 0.15625, ((0, 32),), jnp.float32),
        "first_moment": noise(keys[7], (D, D + HEAD), 1.0, 6.0, ((0, 32),), jnp.float32),
        "second_moment": jnp.clip(jnp.exp(math.log(4.0) - 2.0794415 * jax.random.uniform(keys[8], (D, D + HEAD), jnp.float32) ** levels(keys[8], (D, D + HEAD), ((0, 32),), -0.2, 0.2)), 0.5, 4.0),
    }


beta_one = 0.9
beta_two = 0.999
bias_one = 0.9999734386011124
bias_two = 0.0952078528862911
learn_rate = 0.01
adam_epsilon = 1e-08

def scene_heads(features, bev_scene, lists, slot_ids, w_head):
    cam_count = lists.shape[0]
    slot_cap = lists.shape[2]
    tile_len = bev_scene.shape[0] // cam_count
    offsets = (jnp.arange(cam_count, dtype=jnp.int32) * tile_len)[None, :, None]
    global_cells = (lists.astype(jnp.int32) + offsets).reshape(cam_count * cam_count * slot_cap)
    tables = bev_scene[global_cells].reshape(cam_count, cam_count * slot_cap, bev_scene.shape[1])
    tables = jnp.concatenate([tables, jnp.zeros((cam_count, 1, tables.shape[2]), tables.dtype)], axis=1)
    slots_cam = slot_ids.reshape(cam_count, -1).astype(jnp.int32)
    point_rows = jax.vmap(lambda table_one, slot_one: table_one[slot_one])(tables, slots_cam)
    point_rows = point_rows.reshape(-1, DEPTH, tables.shape[2]).astype(jnp.float32)
    head_out = jnp.dot(features, w_head, preferred_element_type=jnp.float32)
    occupancy = jax.nn.sigmoid(head_out[:, C:])
    context = head_out[:, :C]
    g_context = jnp.einsum('pd,pdc->pc', occupancy, point_rows, precision=lax.Precision.HIGHEST)
    g_occupancy = jnp.einsum('pc,pdc->pd', context, point_rows, precision=lax.Precision.HIGHEST)
    g_logits = occupancy * (1.0 - occupancy) * g_occupancy
    return jnp.concatenate([g_context, g_logits], axis=1).astype(jnp.bfloat16)

def reference(x_in, feat, w_head, g_bev, cell_lists, point_slots, master, first_moment, second_moment):

    def one_scene(items):
        features, bev_scene, lists, slot_ids = items
        return scene_heads(features, bev_scene, lists, slot_ids, w_head)
    g_head = lax.map(one_scene, (feat, g_bev, cell_lists, point_slots))
    g_head = g_head.reshape(-1, g_head.shape[2])
    inputs = x_in.reshape(-1, x_in.shape[2])
    features = feat.reshape(-1, feat.shape[2])
    contract = (((0,), (0,)), ((), ()))
    inner_proj = lax.dot_general(inputs, g_head, contract, preferred_element_type=jnp.float32)
    inner_head = lax.dot_general(features, g_head, contract, preferred_element_type=jnp.float32)
    grad_proj = lax.dot_general(inner_proj, w_head.astype(jnp.float32), (((1,), (1,)), ((), ())), precision=lax.Precision.HIGHEST, preferred_element_type=jnp.float32)
    grad_scale = 1.0 / math.sqrt(SCENES * PIXELS)
    gradient = jnp.concatenate([grad_proj, inner_head], axis=1) * grad_scale
    new_first = beta_one * first_moment + (1.0 - beta_one) * gradient
    new_second = beta_two * second_moment + (1.0 - beta_two) * gradient * gradient
    direction = new_first / bias_one / (jnp.sqrt(new_second / bias_two) + adam_epsilon)
    new_master = master - learn_rate * direction
    return (new_master, new_first, new_second)
```

```python
import functools
import math

import jax
import jax.numpy as jnp
from jax import lax
from jax.experimental import pallas as pl
from jax.experimental.pallas import tpu as pltpu
from jax.sharding import PartitionSpec as P

beta_one = 0.9
beta_two = 0.999
bias_one = 0.9999734386011124
bias_two = 0.0952078528862911
learn_rate = 0.01
adam_epsilon = 1e-08

bf16 = jnp.bfloat16
f32 = jnp.float32
i32 = jnp.int32

NT = (((1,), (1,)), ((), ()))
TN = (((0,), (0,)), ((), ()))

CHIPS = 4
CAP = 512
CH = 128
MIB = 1 << 20


def vmem():
    return pl.BlockSpec(memory_space=pltpu.VMEM)


def smem():
    return pl.BlockSpec(memory_space=pltpu.SMEM)


def split(value):
    high = value.astype(bf16)
    return high, (value - high.astype(f32)).astype(bf16)


def gather_kernel(me_ref, lists_ref, tile_ref, own_ref, pair_ref, one_ref, two_ref, three_ref, wide, rows):
    wide[...] = tile_ref[...].astype(f32)
    me = me_ref[0]
    places = (
        (own_ref, 0), (pair_ref, 0), (one_ref, 0), (one_ref, 1),
        (two_ref, 0), (two_ref, 1), (three_ref, 0), (three_ref, 1),
    )
    for block, (ref, part) in enumerate(places):
        start = jnp.bitwise_xor(me, block) * CAP

        def step(i, carry):
            base = i * 16
            for u in range(16):
                cell = lists_ref[start + base + u]
                rows[pl.ds(base + u, 1), :] = wide[pl.ds(cell, 1), :]
            return carry

        lax.fori_loop(0, CAP // 16, step, 0)
        ref[part] = rows[...].astype(bf16)


def gather_rows(me, lists, tile):
    one = jax.ShapeDtypeStruct((1, CAP, CH), bf16)
    two = jax.ShapeDtypeStruct((2, CAP, CH), bf16)
    return pl.pallas_call(
        gather_kernel,
        out_shape=(one, one, two, two, two),
        in_specs=[smem(), smem(), vmem()],
        out_specs=(vmem(),) * 5,
        scratch_shapes=[pltpu.VMEM(tile.shape, f32), pltpu.VMEM((CAP, CH), f32)],
        compiler_params=pltpu.CompilerParams(vmem_limit_bytes=16 * MIB),
        name="gather_rows",
    )(me, lists, tile)


def weights_kernel(feat_ref, w_ref, slot_ref, wts_ref, occ_ref, ctx_ref):
    block = feat_ref.shape[0]
    head = jnp.dot(feat_ref[...], w_ref[...], preferred_element_type=f32)
    occ_ref[...] = 1.0 / (1.0 + jnp.exp(-head[:, CH:]))
    ctx_ref[:, :CH], ctx_ref[:, CH:] = split(head[:, :CH])
    lane = lax.broadcasted_iota(i32, (8, 128), 1)
    sub = lax.broadcasted_iota(i32, (8, 128), 0)
    half = (lane >= 64).astype(i32)

    def build(i, carry):
        base = pl.multiple_of(i * 16, 16)
        pair = []
        for q in range(2):
            slot = slot_ref[pl.ds(base + q * 8, 8), :]
            occ = occ_ref[pl.ds(base + q * 8, 8), :]
            high = slot >> 8
            low = slot & 255
            occ_high = occ.astype(bf16).astype(f32)
            occ_low = occ - occ_high
            hit = high[None] == lax.broadcasted_iota(i32, (16, 8, 128), 0)
            low_rows = lax.broadcasted_iota(i32, (256, 128), 0)
            left_high, left_low, right = [], [], []
            for j in range(4):
                mine = sub == 2 * j + half
                part_high = jnp.where(mine, occ_high, 0.0)
                part_low = jnp.where(mine, occ_low, 0.0)
                left_high.append(jnp.where(hit, part_high[None], 0.0).reshape(128, 128).astype(bf16))
                left_low.append(jnp.where(hit, part_low[None], 0.0).reshape(128, 128).astype(bf16))
                row = jnp.where(lane[:1] < 64, low[2 * j : 2 * j + 1], low[2 * j + 1 : 2 * j + 2])
                right.append(jnp.where(low_rows == row, 1.0, 0.0).astype(bf16))
            left = jnp.concatenate(
                [jnp.concatenate(left_high, axis=1), jnp.concatenate(left_low, axis=1)], axis=0
            )
            both = lax.dot_general(left, jnp.concatenate(right, axis=1), NT, preferred_element_type=f32)
            pair.append(both[:128] + both[128:])
        for h in range(16):
            rows = slice(h * 8, h * 8 + 8)
            value = jnp.concatenate([pair[0][rows], pair[1][rows]], axis=0)
            columns = slice(h * 256, h * 256 + 256)
            wts_ref[pl.ds(base, 16), columns], wts_ref[pl.ds(block + base, 16), columns] = split(value)
        return carry

    lax.fori_loop(0, block // 16, build, 0)


def pixel_weights(feat, w_wide, slots, block=256):
    pixels, width = feat.shape
    table = 8 * CAP
    return pl.pallas_call(
        weights_kernel,
        grid=(pixels // block,),
        out_shape=(
            jax.ShapeDtypeStruct((2 * pixels, table), bf16),
            jax.ShapeDtypeStruct((pixels, 128), f32),
            jax.ShapeDtypeStruct((pixels, 2 * CH), bf16),
        ),
        in_specs=[
            pl.BlockSpec((block, width), lambda i: (i, 0)),
            pl.BlockSpec((width, 256), lambda i: (0, 0)),
            pl.BlockSpec((block, 128), lambda i: (i, 0)),
        ],
        out_specs=(
            pl.BlockSpec((2 * block, table), lambda i: (i, 0)),
            pl.BlockSpec((block, 128), lambda i: (i, 0)),
            pl.BlockSpec((block, 2 * CH), lambda i: (i, 0)),
        ),
        compiler_params=pltpu.CompilerParams(vmem_limit_bytes=54 * MIB),
        cost_estimate=pl.CostEstimate(flops=25 * 10**9, bytes_accessed=24 * 10**6, transcendentals=0),
        name="pixel_weights",
    )(feat, w_wide, slots)


def grads_kernel(
    own_ref, one_ref, two_ref, three_ref, far_ref, wts_ref, occ_ref, ctx_ref, slot_ref, out_ref, table, scores, picked
):
    block = occ_ref.shape[0]
    count = table.shape[0]

    @pl.when(pl.program_id(0) == 0)
    def _():
        for k, ref in enumerate((own_ref, one_ref, two_ref, three_ref)):
            table[k * CAP : (k + 1) * CAP, :] = ref[0]
        table[4 * CAP :, :] = far_ref[...]

    def score(i, carry):
        start = pl.multiple_of(i * 256, 256)
        rows = table[pl.ds(start, 256), :]
        scores[:, pl.ds(start, 256)] = lax.dot_general(
            ctx_ref[...], jnp.concatenate([rows, rows], axis=1), NT, preferred_element_type=f32
        )
        return carry

    lax.fori_loop(0, count // 256, score, 0, unroll=4)

    def pick(i, carry):
        base = pl.multiple_of(i * 8, 8)
        slot = slot_ref[pl.ds(base, 8), :]
        low = slot & 127
        high = slot >> 7
        total = jnp.zeros((8, 128), f32)
        for g in range(count // 128):
            found = jnp.take_along_axis(
                scores[pl.ds(base, 8), g * 128 : (g + 1) * 128], low, axis=1, mode="promise_in_bounds"
            )
            total = jnp.where(high == g, found, total)
        picked[pl.ds(base, 8), :] = total
        return carry

    lax.fori_loop(0, block // 8, pick, 0, unroll=2)
    both = jnp.dot(wts_ref[...], table[...], preferred_element_type=f32)
    occ = occ_ref[...]
    out_ref[:, :CH] = (both[:block] + both[block:]).astype(bf16)
    out_ref[:, CH:] = (occ * (1.0 - occ) * picked[...]).astype(bf16)


def head_grads(tables, wts, occ, ctx, slots, block=256):
    pixels = occ.shape[0]
    count = 8 * CAP
    first = pl.BlockSpec((1, CAP, CH), lambda i: (0, 0, 0))
    return pl.pallas_call(
        grads_kernel,
        grid=(pixels // block,),
        out_shape=jax.ShapeDtypeStruct((pixels, 256), bf16),
        in_specs=[
            first, first, first, first,
            pl.BlockSpec((4 * CAP, CH), lambda i: (0, 0)),
            pl.BlockSpec((2 * block, count), lambda i: (i, 0)),
            pl.BlockSpec((block, 128), lambda i: (i, 0)),
            pl.BlockSpec((block, 2 * CH), lambda i: (i, 0)),
            pl.BlockSpec((block, 128), lambda i: (i, 0)),
        ],
        out_specs=pl.BlockSpec((block, 256), lambda i: (i, 0)),
        scratch_shapes=[
            pltpu.VMEM((count, CH), bf16),
            pltpu.VMEM((block, count), f32),
            pltpu.VMEM((block, 128), f32),
        ],
        compiler_params=pltpu.CompilerParams(vmem_limit_bytes=54 * MIB),
        name="head_grads",
    )(*tables, wts, occ, ctx, slots)


def inner_kernel(core_ref, x_ref, feat_ref, head_ref, keep_ref, send_ref):
    grads = head_ref[...]
    left = lax.dot_general(x_ref[...], grads, TN, preferred_element_type=f32)
    right = lax.dot_general(feat_ref[...], grads, TN, preferred_element_type=f32)
    lane = lax.broadcasted_iota(i32, (1, 128), 1)
    tail = jnp.where(lane < 64, left[:, CH:], right[:, CH:])
    full = jnp.concatenate([left[:, :CH], right[:, :CH], tail], axis=1)
    owners, half_rows, width = keep_ref.shape
    full = full.reshape(owners, 2, half_rows, width)
    first = core_ref[0] == 0
    keep_ref[...] = jnp.where(first, full[:, 0], full[:, 1])
    send_ref[...] = jnp.where(first, full[:, 1], full[:, 0])


def inner_halves(core, x_in, feat, grads, owners):
    pixels, width = x_in.shape
    step = 384
    half_rows = width // owners // 2
    per_step = step // (2 * half_rows)
    halves = jax.ShapeDtypeStruct((owners, half_rows, 384), f32)
    spec = pl.BlockSpec((per_step, half_rows, 384), lambda i: (i, 0, 0))
    return pl.pallas_call(
        inner_kernel,
        grid=(width // step,),
        out_shape=(halves, halves),
        in_specs=[
            smem(),
            pl.BlockSpec((pixels, step), lambda i: (0, i)),
            pl.BlockSpec((pixels, step), lambda i: (0, i)),
            pl.BlockSpec((pixels, 256), lambda i: (0, 0)),
        ],
        out_specs=(spec, spec),
        compiler_params=pltpu.CompilerParams(vmem_limit_bytes=54 * MIB),
        name="inner_halves",
    )(core, x_in, feat, grads)


def adam_kernel(core_ref, mine_ref, other_ref, w_ref, master_ref, first_ref, second_ref, out_m, out_f, out_s, *, scale):
    mine, other = mine_ref[...], other_ref[...]
    upper = core_ref[0] == 0
    inner = jnp.concatenate([jnp.where(upper, mine, other), jnp.where(upper, other, mine)], axis=0)
    rows = inner.shape[0]
    proj = jnp.concatenate([inner[:, :CH], inner[:, 2 * CH : 2 * CH + 64]], axis=1)
    high = proj.astype(bf16)
    rest = proj - high.astype(f32)
    mid, low = split(rest)
    three = lax.dot_general(
        jnp.concatenate([high, mid, low], axis=0), w_ref[...], NT, preferred_element_type=f32
    )
    wide = three[2 * rows :] + three[rows : 2 * rows] + three[:rows]
    tail = jnp.concatenate([inner[:, CH : 2 * CH], inner[:, 2 * CH + 64 :]], axis=1)
    gradient = jnp.concatenate([wide, tail], axis=1) * scale
    first_new = beta_one * first_ref[...] + (1.0 - beta_one) * gradient
    second_new = beta_two * second_ref[...] + (1.0 - beta_two) * gradient * gradient
    direction = first_new / bias_one / (jnp.sqrt(second_new / bias_two) + adam_epsilon)
    out_m[...] = master_ref[...] - learn_rate * direction
    out_f[...] = first_new
    out_s[...] = second_new


def adam_update(core, mine, other, w_head, master, first, second, scale):
    out = jax.ShapeDtypeStruct(master.shape, f32)
    return pl.pallas_call(
        functools.partial(adam_kernel, scale=scale),
        out_shape=(out, out, out),
        in_specs=[smem()] + [vmem()] * 6,
        out_specs=(vmem(),) * 3,
        compiler_params=pltpu.CompilerParams(vmem_limit_bytes=32 * MIB),
        name="adam_update",
    )(core, mine, other, w_head, master, first, second)


def hop(value, distance):
    return lax.ppermute(value, "cam", [(i, i ^ distance) for i in range(2 * CHIPS)])


def shards(x_in, feat, w_head, g_bev, cell_lists, point_slots, master, first_moment, second_moment):
    cam_count = lax.axis_size("cam")
    data_count = lax.axis_size("dp")
    me = lax.axis_index("cam").astype(i32)
    core = (me & 1).reshape(1)
    features = feat[0]
    pixels = features.shape[0]

    with jax.named_scope("lists"):
        lists = lax.all_to_all(cell_lists[0, 0], "cam", 0, 0, tiled=True)
    own, pair, one, two, three = gather_rows(me.reshape(1), lists.reshape(-1), g_bev[0])
    with jax.named_scope("rows"):
        one, two, three = hop(one, 2), hop(two, 4), hop(three, 6)

    slots = point_slots[0]
    tile = (slots >> 9) ^ me
    slots = jnp.where(slots < 8 * CAP, ((tile & 1) << 11) | ((tile >> 1) << 9) | (slots & (CAP - 1)), 8 * CAP)
    slots = jnp.concatenate([slots, slots], axis=1)
    w_wide = jnp.concatenate([w_head, w_head[:, CH:]], axis=1)
    w_wide, own = lax.optimization_barrier((w_wide, own))
    wts, occ, ctx = pixel_weights(features, w_wide, slots)
    with jax.named_scope("rows_pair"):
        one, two, three, ctx = lax.optimization_barrier((one, two, three, ctx))
        far = hop(jnp.concatenate([pair[0], one[1], two[1], three[1]], axis=0), 1)
    grads = head_grads((own, one, two, three, far), wts, occ, ctx, slots)

    keep, send = inner_halves(core, x_in[0], features, grads, data_count)
    with jax.named_scope("sum_pair"):
        half = (keep + hop(send, 1)).astype(bf16)
    with jax.named_scope("sum_dp"):
        half = lax.all_to_all(half, "dp", 0, 0, tiled=True)
        half = jnp.sum(half.astype(f32), axis=0)
    with jax.named_scope("sum_x"):
        half = (half + hop(half, 2)) + (hop(half, 4) + hop(half, 6))
    with jax.named_scope("share_pair"):
        other = hop(half, 1)
    scale = 1.0 / math.sqrt(data_count * cam_count * pixels)
    return adam_update(core, half, other, w_head, master, first_moment, second_moment, scale)


def solution(mesh):
    placed = (
        P("dp", "cam", None),
        P("dp", "cam", None),
        P(),
        P("dp", "cam", None),
        P("dp", "cam", None, None),
        P("dp", "cam", None),
        P("dp", None),
        P("dp", None),
        P("dp", None),
    )
    return jax.shard_map(
        shards,
        mesh=mesh,
        in_specs=placed,
        out_specs=(P("dp", None), P("dp", None), P("dp", None)),
        check_vma=False,
    )
```

```python
import functools
import math

import jax
import jax.numpy as jnp
from jax import lax
from jax.experimental import pallas as pl
from jax.experimental.pallas import tpu as pltpu
from jax.sharding import PartitionSpec as P

beta_one = 0.9
beta_two = 0.999
bias_one = 0.9999734386011124
bias_two = 0.0952078528862911
learn_rate = 0.01
adam_epsilon = 1e-08

bf16 = jnp.bfloat16
f32 = jnp.float32
i32 = jnp.int32

NT = (((1,), (1,)), ((), ()))
TN = (((0,), (0,)), ((), ()))

CHIPS = 4
CAP = 512
CH = 128
MIB = 1 << 20


def vmem():
    return pl.BlockSpec(memory_space=pltpu.VMEM)


def smem():
    return pl.BlockSpec(memory_space=pltpu.SMEM)


def split(value):
    high = value.astype(bf16)
    return high, (value - high.astype(f32)).astype(bf16)


def gather_kernel(me_ref, lists_ref, tile_ref, own_ref, pair_ref, one_ref, two_ref, three_ref, wide, rows):
    wide[...] = tile_ref[...].astype(f32)
    me = me_ref[0]
    places = (
        (own_ref, 0), (pair_ref, 0), (one_ref, 0), (one_ref, 1),
        (two_ref, 0), (two_ref, 1), (three_ref, 0), (three_ref, 1),
    )
    for block, (ref, part) in enumerate(places):
        start = jnp.bitwise_xor(me, block) * CAP

        def step(i, carry):
            base = i * 16
            for u in range(16):
                cell = lists_ref[start + base + u]
                rows[pl.ds(base + u, 1), :] = wide[pl.ds(cell, 1), :]
            return carry

        lax.fori_loop(0, CAP // 16, step, 0)
        ref[part] = rows[...].astype(bf16)


def gather_rows(me, lists, tile):
    one = jax.ShapeDtypeStruct((1, CAP, CH), bf16)
    two = jax.ShapeDtypeStruct((2, CAP, CH), bf16)
    return pl.pallas_call(
        gather_kernel,
        out_shape=(one, one, two, two, two),
        in_specs=[smem(), smem(), vmem()],
        out_specs=(vmem(),) * 5,
        scratch_shapes=[pltpu.VMEM(tile.shape, f32), pltpu.VMEM((CAP, CH), f32)],
        compiler_params=pltpu.CompilerParams(vmem_limit_bytes=16 * MIB),
        name="gather_rows",
    )(me, lists, tile)


def weights_kernel(me_ref, feat_ref, w_ref, slot_ref, wts_ref, occ_ref, ctx_ref, place_ref):
    block = feat_ref.shape[0]
    head = lax.dot_general(feat_ref[...], w_ref[...], NT, preferred_element_type=f32)
    ctx_ref[:, :CH], ctx_ref[:, CH:] = split(head[:, :CH])
    occ = 1.0 / (1.0 + jnp.exp(-head[:, CH:]))
    occ_ref[...] = jnp.concatenate([occ, occ], axis=1)
    slots = slot_ref[...]
    tile = (slots >> 9) ^ me_ref[0]
    slots = jnp.where(slots < 8 * CAP, ((tile & 1) << 11) | ((tile >> 1) << 9) | (slots & (CAP - 1)), 8 * CAP)
    place_ref[...] = jnp.concatenate([slots, slots], axis=1)
    lane = lax.broadcasted_iota(i32, (1, 128), 1)
    lane16 = lax.broadcasted_iota(i32, (16, 128), 1)
    sub16 = lax.broadcasted_iota(i32, (16, 128), 0)
    half16 = (lane16 >= 64).astype(i32)
    masks = [((sub16 & 7) == 2 * j + half16).astype(f32).astype(bf16) for j in range(4)]
    low_rows = [(sub16 + 16 * t).astype(f32).astype(bf16) for t in range(16)]
    zero = jnp.zeros((16, 128), bf16)
    one = jnp.ones((16, 128), bf16)

    def build(i, carry):
        base = pl.multiple_of(i * 16, 16)
        pair = []
        for q in range(2):
            slot = place_ref[pl.ds(base + q * 8, 8), :]
            occ = occ_ref[pl.ds(base + q * 8, 8), :]
            high = (slot >> 8).astype(f32)
            low = (slot & 255).astype(f32)
            key = jnp.concatenate([high, high - 1.0], axis=0).astype(bf16)
            hits = [key == jnp.asarray(2.0 * t, bf16) for t in range(8)]
            occ_high, occ_low = split(jnp.concatenate([occ, occ], axis=0))
            left_high, left_low, right = [], [], []
            for j in range(4):
                part_high = occ_high * masks[j]
                part_low = occ_low * masks[j]
                left_high.append(jnp.concatenate([jnp.where(hit, part_high, zero) for hit in hits], axis=0))
                left_low.append(jnp.concatenate([jnp.where(hit, part_low, zero) for hit in hits], axis=0))
                row = jnp.where(lane < 64, low[2 * j : 2 * j + 1], low[2 * j + 1 : 2 * j + 2])
                row = jnp.broadcast_to(row, (16, 128)).astype(bf16)
                right.append(jnp.concatenate([jnp.where(rows == row, one, zero) for rows in low_rows], axis=0))
            left = jnp.concatenate(
                [jnp.concatenate(left_high, axis=1), jnp.concatenate(left_low, axis=1)], axis=0
            )
            both = lax.dot_general(left, jnp.concatenate(right, axis=1), NT, preferred_element_type=f32)
            pair.append(both[:128] + both[128:])
        for h in range(16):
            rows = slice(h * 8, h * 8 + 8)
            value = jnp.concatenate([pair[0][rows], pair[1][rows]], axis=0)
            columns = slice(h * 256, h * 256 + 256)
            wts_ref[pl.ds(base, 16), columns], wts_ref[pl.ds(block + base, 16), columns] = split(value)
        return carry

    lax.fori_loop(0, block // 16, build, 0, unroll=8)


def pixel_weights(me, feat, w_head, slots, block=256):
    pixels, width = feat.shape
    depth = slots.shape[1]
    table = 8 * CAP
    return pl.pallas_call(
        weights_kernel,
        grid=(pixels // block,),
        out_shape=(
            jax.ShapeDtypeStruct((2 * pixels, table), bf16),
            jax.ShapeDtypeStruct((pixels, 128), f32),
            jax.ShapeDtypeStruct((pixels, 2 * CH), bf16),
            jax.ShapeDtypeStruct((pixels, 128), i32),
        ),
        in_specs=[
            smem(),
            pl.BlockSpec((block, width), lambda i: (i, 0)),
            pl.BlockSpec(w_head.shape, lambda i: (0, 0)),
            pl.BlockSpec((block, depth), lambda i: (i, 0)),
        ],
        out_specs=(
            pl.BlockSpec((2 * block, table), lambda i: (i, 0)),
            pl.BlockSpec((block, 128), lambda i: (i, 0)),
            pl.BlockSpec((block, 2 * CH), lambda i: (i, 0)),
            pl.BlockSpec((block, 128), lambda i: (i, 0)),
        ),
        compiler_params=pltpu.CompilerParams(vmem_limit_bytes=50 * MIB),
        cost_estimate=pl.CostEstimate(flops=20 * 10**9, bytes_accessed=24 * 10**6, transcendentals=0),
        name="pixel_weights",
    )(me, feat, w_head, slots)


def grads_kernel(
    core_ref, own_ref, one_ref, two_ref, three_ref, far_ref, wts_ref, occ_ref, place_ref, ctx_ref, x_hbm, feat_hbm,
    keep_ref, send_ref, table, flip, scores, mixed, picked, head, x_in, feat, sems,
):
    step = pl.program_id(0)
    last = pl.num_programs(0) - 1
    block = occ_ref.shape[0]
    count = table.shape[0]
    chunks = count // 256
    x_copy = pltpu.make_async_copy(x_hbm, x_in, sems.at[0])
    feat_copy = pltpu.make_async_copy(feat_hbm, feat, sems.at[1])

    def score(i):
        columns = pl.ds(pl.multiple_of(i * 256, 256), 256)
        part = flip[:, columns]
        scores[step % 2, :, columns] = jnp.dot(
            ctx_ref[...], jnp.concatenate([part, part], axis=0), preferred_element_type=f32
        )

    def pick(i):
        old = (step + 1) % 2
        for q in range(block // chunks // 8):
            base = pl.multiple_of(i * (block // chunks), 8) + q * 8
            place = place_ref[pl.ds(base, 8), :]
            low = place & 127
            high = place >> 7
            total = jnp.zeros((8, 128), f32)
            for g in range(count // 128):
                found = jnp.take_along_axis(
                    scores[old, pl.ds(base, 8), g * 128 : (g + 1) * 128], low, axis=1, mode="promise_in_bounds"
                )
                total = jnp.where(high == g, found, total)
            picked[pl.ds(base, 8), :] = total

    def mix(i):
        rows = pl.ds(pl.multiple_of(i * 256, 256), 256)
        mixed[...] += jnp.dot(wts_ref[:, rows], table[rows, :], preferred_element_type=f32)

    def finish():
        rows = pl.ds(pl.multiple_of((step - 1) * block, block), block)
        occ = occ_ref[...]
        head[rows, :CH] = (mixed[:block] + mixed[block:]).astype(bf16)
        head[rows, CH:] = (occ * (1.0 - occ) * picked[...]).astype(bf16)

    @pl.when(step == 0)
    def _():
        x_copy.start()
        feat_copy.start()
        for k, ref in enumerate((own_ref, one_ref, two_ref, three_ref)):
            table[k * CAP : (k + 1) * CAP, :] = ref[0]
        table[4 * CAP :, :] = far_ref[...]

        def body(i, carry):
            rows = pl.ds(pl.multiple_of(i * 256, 256), 256)
            flip[:, rows] = table[rows, :].T
            score(i)
            return carry

        lax.fori_loop(0, chunks, body, 0, unroll=8)

    @pl.when((step > 0) & (step < last))
    def _():
        mixed[...] = jnp.zeros_like(mixed)

        def body(i, carry):
            score(i)
            pick(i)
            mix(i)
            return carry

        lax.fori_loop(0, chunks, body, 0, unroll=8)
        finish()

    @pl.when(step == last)
    def _():
        mixed[...] = jnp.zeros_like(mixed)

        def body(i, carry):
            pick(i)
            mix(i)
            return carry

        lax.fori_loop(0, chunks, body, 0, unroll=8)
        finish()
        x_copy.wait()
        feat_copy.wait()
        owners, half_rows, width = keep_ref.shape
        span = 384
        per_span = span // (2 * half_rows)
        grads = head[...]
        lane = lax.broadcasted_iota(i32, (1, 128), 1)
        first = core_ref[0] == 0
        for n in range(x_in.shape[1] // span):
            columns = slice(n * span, (n + 1) * span)
            left = lax.dot_general(x_in[:, columns], grads, TN, preferred_element_type=f32)
            right = lax.dot_general(feat[:, columns], grads, TN, preferred_element_type=f32)
            tail = jnp.where(lane < 64, left[:, CH:], right[:, CH:])
            full = jnp.concatenate([left[:, :CH], right[:, :CH], tail], axis=1)
            full = full.reshape(per_span, 2, half_rows, width)
            part = slice(n * per_span, (n + 1) * per_span)
            keep_ref[part] = jnp.where(first, full[:, 0], full[:, 1])
            send_ref[part] = jnp.where(first, full[:, 1], full[:, 0])


def inner_halves(core, tables, wts, occ, places, ctx, x_in, feat, owners, block=256):
    pixels, width = feat.shape
    count = 8 * CAP
    blocks = pixels // block
    first = pl.BlockSpec((1, CAP, CH), lambda i: (0, 0, 0))
    halves = jax.ShapeDtypeStruct((owners, width // owners // 2, 384), f32)

    def behind(i):
        return (jnp.maximum(i - 1, 0), 0)

    return pl.pallas_call(
        grads_kernel,
        grid=(blocks + 1,),
        out_shape=(halves, halves),
        in_specs=[
            smem(),
            first, first, first, first,
            pl.BlockSpec((4 * CAP, CH), lambda i: (0, 0)),
            pl.BlockSpec((2 * block, count), behind),
            pl.BlockSpec((block, 128), behind),
            pl.BlockSpec((block, 128), behind),
            pl.BlockSpec((block, 2 * CH), lambda i: (jnp.minimum(i, blocks - 1), 0)),
            pl.BlockSpec(memory_space=pl.ANY),
            pl.BlockSpec(memory_space=pl.ANY),
        ],
        out_specs=(vmem(), vmem()),
        scratch_shapes=[
            pltpu.VMEM((count, CH), bf16),
            pltpu.VMEM((CH, count), bf16),
            pltpu.VMEM((2, block, count), f32),
            pltpu.VMEM((2 * block, CH), f32),
            pltpu.VMEM((block, 128), f32),
            pltpu.VMEM((pixels, 256), bf16),
            pltpu.VMEM((pixels, width), bf16),
            pltpu.VMEM((pixels, width), bf16),
            pltpu.SemaphoreType.DMA((2,)),
        ],
        compiler_params=pltpu.CompilerParams(vmem_limit_bytes=50 * MIB),
        name="inner_halves",
    )(core, *tables, wts, occ, places, ctx, x_in, feat)


def adam_kernel(core_ref, mine_ref, other_ref, w_ref, master_ref, first_ref, second_ref, out_m, out_f, out_s, *, scale):
    mine, other = mine_ref[...], other_ref[...]
    upper = core_ref[0] == 0
    inner = jnp.concatenate([jnp.where(upper, mine, other), jnp.where(upper, other, mine)], axis=0)
    rows = inner.shape[0]
    proj = jnp.concatenate([inner[:, :CH], inner[:, 2 * CH : 2 * CH + 64]], axis=1)
    high = proj.astype(bf16)
    rest = proj - high.astype(f32)
    mid, low = split(rest)
    three = jnp.dot(jnp.concatenate([high, mid, low], axis=0), w_ref[...], preferred_element_type=f32)
    wide = three[2 * rows :] + three[rows : 2 * rows] + three[:rows]
    tail = jnp.concatenate([inner[:, CH : 2 * CH], inner[:, 2 * CH + 64 :]], axis=1)
    gradient = jnp.concatenate([wide, tail], axis=1) * scale
    first_new = beta_one * first_ref[...] + (1.0 - beta_one) * gradient
    second_new = beta_two * second_ref[...] + (1.0 - beta_two) * gradient * gradient
    direction = first_new / bias_one / (jnp.sqrt(second_new / bias_two) + adam_epsilon)
    out_m[...] = master_ref[...] - learn_rate * direction
    out_f[...] = first_new
    out_s[...] = second_new


def adam_update(core, mine, other, w_head, master, first, second, scale):
    out = jax.ShapeDtypeStruct(master.shape, f32)
    return pl.pallas_call(
        functools.partial(adam_kernel, scale=scale),
        out_shape=(out, out, out),
        in_specs=[smem()] + [vmem()] * 6,
        out_specs=(vmem(),) * 3,
        compiler_params=pltpu.CompilerParams(vmem_limit_bytes=32 * MIB),
        name="adam_update",
    )(core, mine, other, w_head, master, first, second)


def hop(value, distance):
    return lax.ppermute(value, "cam", [(i, i ^ distance) for i in range(2 * CHIPS)])


def shards(x_in, feat, w_head, g_bev, cell_lists, point_slots, master, first_moment, second_moment):
    cam_count = lax.axis_size("cam")
    data_count = lax.axis_size("dp")
    me = lax.axis_index("cam").astype(i32)
    core = (me & 1).reshape(1)
    features = feat[0]
    pixels = features.shape[0]
    w_head = w_head.T

    with jax.named_scope("lists"):
        lists = lax.all_to_all(cell_lists[0, 0], "cam", 0, 0, tiled=True)
    own, pair, one, two, three = gather_rows(me.reshape(1), lists.reshape(-1), g_bev[0])
    with jax.named_scope("rows"):
        one, two, three = hop(one, 2), hop(two, 4), hop(three, 6)

    w_head_late, own = lax.optimization_barrier((w_head, own))
    wts, occ, ctx, places = pixel_weights(me.reshape(1), features, w_head_late, point_slots[0])
    with jax.named_scope("rows_pair"):
        one, two, three, ctx = lax.optimization_barrier((one, two, three, ctx))
        far = hop(jnp.concatenate([pair[0], one[1], two[1], three[1]], axis=0), 1)
    keep, send = inner_halves(
        core, (own, one, two, three, far), wts, occ, places, ctx, x_in[0], features, data_count
    )
    with jax.named_scope("sum_pair"):
        half = (keep + hop(send, 1)).astype(bf16)
    with jax.named_scope("sum_dp"):
        half = lax.all_to_all(half, "dp", 0, 0, tiled=True)
        half = jnp.sum(half.astype(f32), axis=0)
    with jax.named_scope("sum_x"):
        half = (half + hop(half, 2)) + (hop(half, 4) + hop(half, 6))
    with jax.named_scope("share_pair"):
        other = hop(half, 1)
    scale = 1.0 / math.sqrt(data_count * cam_count * pixels)
    return adam_update(core, half, other, w_head, master, first_moment, second_moment, scale)


def solution(mesh):
    placed = (
        P("dp", "cam", None),
        P("dp", "cam", None),
        P(),
        P("dp", "cam", None),
        P("dp", "cam", None, None),
        P("dp", "cam", None),
        P("dp", None),
        P("dp", None),
        P("dp", None),
    )
    return jax.shard_map(
        shards,
        mesh=mesh,
        in_specs=placed,
        out_specs=(P("dp", None), P("dp", None), P("dp", None)),
        check_vma=False,
    )
```

```python
import functools
import math

import jax
import jax.numpy as jnp
from jax import lax
from jax.experimental import pallas as pl
from jax.experimental.pallas import tpu as pltpu
from jax.sharding import PartitionSpec as P

beta_one = 0.9
beta_two = 0.999
bias_one = 0.9999734386011124
bias_two = 0.0952078528862911
learn_rate = 0.01
adam_epsilon = 1e-08

bf16 = jnp.bfloat16
f32 = jnp.float32
i32 = jnp.int32

NT = (((1,), (1,)), ((), ()))
TN = (((0,), (0,)), ((), ()))

CHIPS = 4
CAP = 512
CH = 128
SUMS = 128
MIB = 1 << 20


def vmem():
    return pl.BlockSpec(memory_space=pltpu.VMEM)


def smem():
    return pl.BlockSpec(memory_space=pltpu.SMEM)


def split(value):
    high = value.astype(bf16)
    return high, (value - high.astype(f32)).astype(bf16)


def gather_kernel(me_ref, lists_ref, tile_ref, own_ref, pair_ref, one_ref, two_ref, three_ref, wide, rows):
    wide[...] = tile_ref[...].astype(f32)
    me = me_ref[0]
    places = (
        (own_ref, 0), (pair_ref, 0), (one_ref, 0), (one_ref, 1),
        (two_ref, 0), (two_ref, 1), (three_ref, 0), (three_ref, 1),
    )
    for block, (ref, part) in enumerate(places):
        start = jnp.bitwise_xor(me, block) * CAP

        def step(i, carry):
            base = i * 16
            for u in range(16):
                cell = lists_ref[start + base + u]
                rows[pl.ds(base + u, 1), :] = wide[pl.ds(cell, 1), :]
            return carry

        lax.fori_loop(0, CAP // 16, step, 0)
        ref[part] = rows[...].astype(bf16)


def gather_rows(me, lists, tile):
    one = jax.ShapeDtypeStruct((1, CAP, CH), bf16)
    two = jax.ShapeDtypeStruct((2, CAP, CH), bf16)
    return pl.pallas_call(
        gather_kernel,
        out_shape=(one, one, two, two, two),
        in_specs=[smem(), smem(), vmem()],
        out_specs=(vmem(),) * 5,
        scratch_shapes=[pltpu.VMEM(tile.shape, f32), pltpu.VMEM((CAP, CH), f32)],
        compiler_params=pltpu.CompilerParams(vmem_limit_bytes=16 * MIB),
        name="gather_rows",
    )(me, lists, tile)


def head_kernel(me_ref, feat_ref, w_ref, slot_ref, occ_ref, ctx_ref, place_ref):
    head = lax.dot_general(feat_ref[...], w_ref[...], NT, preferred_element_type=f32)
    ctx_ref[:, :CH], ctx_ref[:, CH:] = split(head[:, :CH])
    occ = 1.0 / (1.0 + jnp.exp(-head[:, CH:]))
    occ_ref[...] = jnp.concatenate([occ, occ], axis=1)
    slots = slot_ref[...].T
    tile = (slots >> 9) ^ me_ref[0]
    slots = jnp.where(slots < 8 * CAP, ((tile & 1) << 11) | ((tile >> 1) << 9) | (slots & (CAP - 1)), 8 * CAP)
    place_ref[...] = jnp.concatenate([slots, slots], axis=1)


def head_values(me, feat, w_head, slots, block=256):
    pixels, width = feat.shape

    def rows(height, lanes):
        return pl.BlockSpec((height, lanes), lambda i: (i, 0))

    return pl.pallas_call(
        head_kernel,
        grid=(pixels // block,),
        out_shape=(
            jax.ShapeDtypeStruct((pixels, 128), f32),
            jax.ShapeDtypeStruct((pixels, 2 * CH), bf16),
            jax.ShapeDtypeStruct((pixels, 128), i32),
        ),
        in_specs=[
            smem(),
            rows(block, width),
            pl.BlockSpec(w_head.shape, lambda i: (0, 0)),
            pl.BlockSpec((slots.shape[0], block), lambda i: (0, i)),
        ],
        out_specs=(rows(block, 128), rows(block, 2 * CH), rows(block, 128)),
        compiler_params=pltpu.CompilerParams(vmem_limit_bytes=60 * MIB),
        cost_estimate=pl.CostEstimate(flops=4 * 10**9, bytes_accessed=8 * 10**6, transcendentals=0),
        name="head_values",
    )(me, feat, w_head, slots)


def weights_kernel(*refs):
    occ_ref, place_ref, wts_ref, token_ref = refs[-4:]
    block = occ_ref.shape[0]
    token_ref[...] = jnp.zeros_like(token_ref)
    lane = lax.broadcasted_iota(i32, (1, 128), 1)
    lane16 = lax.broadcasted_iota(i32, (16, 128), 1)
    sub16 = lax.broadcasted_iota(i32, (16, 128), 0)
    half16 = (lane16 >= 64).astype(i32)
    masks = [((sub16 & 7) == 2 * j + half16).astype(f32).astype(bf16) for j in range(4)]
    low_rows = [(sub16 + 16 * t).astype(f32).astype(bf16) for t in range(16)]
    zero = jnp.zeros((16, 128), bf16)
    one = jnp.ones((16, 128), bf16)

    def build(i, carry):
        base = pl.multiple_of(i * 16, 16)
        pair = []
        for q in range(2):
            slot = place_ref[pl.ds(base + q * 8, 8), :]
            occ = occ_ref[pl.ds(base + q * 8, 8), :]
            high = (slot >> 8).astype(f32)
            low = (slot & 255).astype(f32)
            key = jnp.concatenate([high, high - 1.0], axis=0).astype(bf16)
            hits = [key == jnp.asarray(2.0 * t, bf16) for t in range(8)]
            occ_high, occ_low = split(jnp.concatenate([occ, occ], axis=0))
            left_high, left_low, right = [], [], []
            for j in range(4):
                part_high = occ_high * masks[j]
                part_low = occ_low * masks[j]
                left_high.append(jnp.concatenate([jnp.where(hit, part_high, zero) for hit in hits], axis=0))
                left_low.append(jnp.concatenate([jnp.where(hit, part_low, zero) for hit in hits], axis=0))
                row = jnp.where(lane < 64, low[2 * j : 2 * j + 1], low[2 * j + 1 : 2 * j + 2])
                row = jnp.broadcast_to(row, (16, 128)).astype(bf16)
                right.append(jnp.concatenate([jnp.where(rows == row, one, zero) for rows in low_rows], axis=0))
            left = jnp.concatenate(
                [jnp.concatenate(left_high, axis=1), jnp.concatenate(left_low, axis=1)], axis=0
            )
            both = lax.dot_general(left, jnp.concatenate(right, axis=1), NT, preferred_element_type=f32)
            pair.append(both[:128] + both[128:])
        for h in range(16):
            rows = slice(h * 8, h * 8 + 8)
            value = jnp.concatenate([pair[0][rows], pair[1][rows]], axis=0)
            columns = slice(h * 256, h * 256 + 256)
            wts_ref[pl.ds(base, 16), columns], wts_ref[pl.ds(block + base, 16), columns] = split(value)
        return carry

    lax.fori_loop(0, block // 16, build, 0, unroll=8)


def pixel_weights(after, occ, places, first, count, wts=None, block=SUMS):
    pixels = occ.shape[0]
    table = 8 * CAP
    operands = tuple(after) if wts is None else (wts, *after)
    return pl.pallas_call(
        weights_kernel,
        grid=(count,),
        out_shape=(jax.ShapeDtypeStruct((2 * pixels, table), bf16), jax.ShapeDtypeStruct((8, 128), f32)),
        in_specs=[pl.BlockSpec(memory_space=pl.ANY)] * len(operands)
        + [pl.BlockSpec((block, 128), lambda i: (i + first, 0))] * 2,
        out_specs=(
            pl.BlockSpec((2 * block, table), lambda i: (i + first, 0)),
            pl.BlockSpec((8, 128), lambda i: (0, 0)),
        ),
        input_output_aliases={} if wts is None else {0: 0},
        compiler_params=pltpu.CompilerParams(vmem_limit_bytes=50 * MIB),
        cost_estimate=pl.CostEstimate(flops=25 * 10**8 * count, bytes_accessed=3 * 10**6 * count, transcendentals=0),
        name="pixel_weights",
    )(*operands, occ, places)


def grads_kernel(
    core_ref, own_ref, one_ref, two_ref, three_ref, far_ref, wts_ref, occ_ref, place_ref, ctx_ref, x_hbm, feat_hbm,
    keep_ref, send_ref, table, flip, scores, mixed, picked, head, x_in, feat, sems, *, owners,
):
    step = pl.program_id(0)
    last = pl.num_programs(0) - 1
    block = occ_ref.shape[0]
    count = table.shape[0]
    chunks = count // 256
    x_copy = pltpu.make_async_copy(x_hbm, x_in, sems.at[0])
    feat_copy = pltpu.make_async_copy(feat_hbm, feat, sems.at[1])

    def score(i):
        columns = pl.ds(pl.multiple_of(i * 256, 256), 256)
        part = flip[:, columns]
        scores[step % 2, :, columns] = jnp.dot(
            ctx_ref[...], jnp.concatenate([part, part], axis=0), preferred_element_type=f32
        )

    def pick(i):
        old = (step + 1) % 2
        for q in range(block // chunks // 8):
            base = pl.multiple_of(i * (block // chunks), 8) + q * 8
            place = place_ref[pl.ds(base, 8), :]
            low = place & 127
            high = place >> 7
            total = jnp.zeros((8, 128), f32)
            for g in range(count // 128):
                found = jnp.take_along_axis(
                    scores[old, pl.ds(base, 8), g * 128 : (g + 1) * 128], low, axis=1, mode="promise_in_bounds"
                )
                total = jnp.where(high == g, found, total)
            picked[pl.ds(base, 8), :] = total

    def mix(i):
        rows = pl.ds(pl.multiple_of(i * 256, 256), 256)
        mixed[...] += jnp.dot(wts_ref[:, rows], table[rows, :], preferred_element_type=f32)

    def finish():
        rows = pl.ds(pl.multiple_of((step - 1) * block, block), block)
        occ = occ_ref[...]
        both = mixed[...].reshape(block // SUMS, 2, SUMS, CH)
        head[rows, :CH] = (both[:, 0] + both[:, 1]).reshape(block, CH).astype(bf16)
        head[rows, CH:] = (occ * (1.0 - occ) * picked[...]).astype(bf16)

    @pl.when(step == 0)
    def _():
        x_copy.start()
        feat_copy.start()
        for k, ref in enumerate((own_ref, one_ref, two_ref, three_ref)):
            table[k * CAP : (k + 1) * CAP, :] = ref[0]
        table[4 * CAP :, :] = far_ref[...]

        def body(i, carry):
            rows = pl.ds(pl.multiple_of(i * 256, 256), 256)
            flip[:, rows] = table[rows, :].T
            score(i)
            return carry

        lax.fori_loop(0, chunks, body, 0, unroll=8)

    @pl.when((step > 0) & (step < last))
    def _():
        mixed[...] = jnp.zeros_like(mixed)

        def body(i, carry):
            score(i)
            pick(i)
            mix(i)
            return carry

        lax.fori_loop(0, chunks, body, 0, unroll=8)
        finish()

    @pl.when(step == last)
    def _():
        mixed[...] = jnp.zeros_like(mixed)

        def body(i, carry):
            pick(i)
            mix(i)
            return carry

        lax.fori_loop(0, chunks, body, 0, unroll=8)
        finish()
        x_copy.wait()
        feat_copy.wait()
        rows, width = keep_ref.shape
        half_rows = rows // owners
        span = 384
        per_span = span // (2 * half_rows)
        grads = head[...]
        lane = lax.broadcasted_iota(i32, (1, 128), 1)
        first = core_ref[0] == 0
        for n in range(x_in.shape[1] // span):
            columns = slice(n * span, (n + 1) * span)
            left = lax.dot_general(x_in[:, columns], grads, TN, preferred_element_type=f32)
            right = lax.dot_general(feat[:, columns], grads, TN, preferred_element_type=f32)
            tail = jnp.where(lane < 64, left[:, CH:], right[:, CH:])
            full = jnp.concatenate([left[:, :CH], right[:, :CH], tail], axis=1)
            full = full.reshape(per_span, 2, half_rows, width)
            height = per_span * half_rows
            part = slice(n * height, (n + 1) * height)
            keep_ref[part] = jnp.where(first, full[:, 0], full[:, 1]).reshape(height, width)
            send_ref[part] = jnp.where(first, full[:, 1], full[:, 0]).reshape(height, width).astype(bf16)


def inner_halves(core, tables, wts, occ, places, ctx, x_in, feat, owners, block=256):
    pixels, width = feat.shape
    count = 8 * CAP
    blocks = pixels // block
    first = pl.BlockSpec((1, CAP, CH), lambda i: (0, 0, 0))
    half = (width // 2, 384)

    def behind(i):
        return (jnp.maximum(i - 1, 0), 0)

    return pl.pallas_call(
        functools.partial(grads_kernel, owners=owners),
        grid=(blocks + 1,),
        out_shape=(jax.ShapeDtypeStruct(half, f32), jax.ShapeDtypeStruct(half, bf16)),
        in_specs=[
            smem(),
            first, first, first, first,
            pl.BlockSpec((4 * CAP, CH), lambda i: (0, 0)),
            pl.BlockSpec((2 * block, count), behind),
            pl.BlockSpec((block, 128), behind),
            pl.BlockSpec((block, 128), behind),
            pl.BlockSpec((block, 2 * CH), lambda i: (jnp.minimum(i, blocks - 1), 0)),
            pl.BlockSpec(memory_space=pl.ANY),
            pl.BlockSpec(memory_space=pl.ANY),
        ],
        out_specs=(vmem(), vmem()),
        scratch_shapes=[
            pltpu.VMEM((count, CH), bf16),
            pltpu.VMEM((CH, count), bf16),
            pltpu.VMEM((2, block, count), f32),
            pltpu.VMEM((2 * block, CH), f32),
            pltpu.VMEM((block, 128), f32),
            pltpu.VMEM((pixels, 256), bf16),
            pltpu.VMEM((pixels, width), bf16),
            pltpu.VMEM((pixels, width), bf16),
            pltpu.SemaphoreType.DMA((2,)),
        ],
        compiler_params=pltpu.CompilerParams(vmem_limit_bytes=50 * MIB),
        name="inner_halves",
    )(core, *tables, wts, occ, places, ctx, x_in, feat)


def adam_kernel(core_ref, mine_ref, other_ref, w_ref, master_ref, first_ref, second_ref, out_m, out_f, out_s, *, scale):
    mine, other = mine_ref[...], other_ref[...]
    upper = core_ref[0] == 0
    inner = jnp.concatenate([jnp.where(upper, mine, other), jnp.where(upper, other, mine)], axis=0)
    rows = inner.shape[0]
    proj = jnp.concatenate([inner[:, :CH], inner[:, 2 * CH : 2 * CH + 64]], axis=1)
    high = proj.astype(bf16)
    rest = proj - high.astype(f32)
    mid, low = split(rest)
    three = jnp.dot(jnp.concatenate([high, mid, low], axis=0), w_ref[...], preferred_element_type=f32)
    wide = three[2 * rows :] + three[rows : 2 * rows] + three[:rows]
    tail = jnp.concatenate([inner[:, CH : 2 * CH], inner[:, 2 * CH + 64 :]], axis=1)
    gradient = jnp.concatenate([wide, tail], axis=1) * scale
    first_new = beta_one * first_ref[...] + (1.0 - beta_one) * gradient
    second_new = beta_two * second_ref[...] + (1.0 - beta_two) * gradient * gradient
    direction = first_new / bias_one / (jnp.sqrt(second_new / bias_two) + adam_epsilon)
    out_m[...] = master_ref[...] - learn_rate * direction
    out_f[...] = first_new
    out_s[...] = second_new


def adam_update(core, mine, other, w_head, master, first, second, scale):
    out = jax.ShapeDtypeStruct(master.shape, f32)
    return pl.pallas_call(
        functools.partial(adam_kernel, scale=scale),
        out_shape=(out, out, out),
        in_specs=[smem()] + [vmem()] * 6,
        out_specs=(vmem(),) * 3,
        compiler_params=pltpu.CompilerParams(vmem_limit_bytes=32 * MIB),
        name="adam_update",
    )(core, mine, other, w_head, master, first, second)


def hop(value, distance):
    return lax.ppermute(value, "cam", [(i, i ^ distance) for i in range(2 * CHIPS)])


def shards(x_in, feat, w_head, g_bev, cell_lists, point_slots, master, first_moment, second_moment):
    cam_count = lax.axis_size("cam")
    data_count = lax.axis_size("dp")
    me = lax.axis_index("cam").astype(i32)
    core = (me & 1).reshape(1)
    features = feat[0]
    pixels = features.shape[0]
    w_head = w_head.T

    with jax.named_scope("lists"):
        lists = lax.all_to_all(cell_lists[0, 0], "cam", 0, 0, tiled=True)
    occ, ctx, places = head_values(me.reshape(1), features, w_head, point_slots[0].T)
    own, pair, one, two, three = gather_rows(me.reshape(1), lists.reshape(-1), g_bev[0])
    with jax.named_scope("rows"):
        one, two, three = hop(one, 2), hop(two, 4), hop(three, 6)
    wts, token = pixel_weights((own,), occ, places, 0, pixels // SUMS - 1)
    with jax.named_scope("rows_pair"):
        one, two, three, token = lax.optimization_barrier((one, two, three, token))
        far = hop(jnp.concatenate([pair[0], one[1], two[1], three[1]], axis=0), 1)
    wts, _ = pixel_weights((token,), occ, places, pixels // SUMS - 1, 1, wts)
    keep, send = inner_halves(
        core, (own, one, two, three, far), wts, occ, places, ctx, x_in[0], features, data_count
    )
    with jax.named_scope("sum_pair"):
        half = (keep + hop(send, 1).astype(f32)).astype(bf16)
        half = half.reshape(data_count, -1, half.shape[1])
    with jax.named_scope("sum_dp"):
        half = lax.all_to_all(half, "dp", 0, 0, tiled=True)
        half = jnp.sum(half.astype(f32), axis=0)
    with jax.named_scope("sum_x"):
        half = (half + hop(half, 2)) + (hop(half, 4) + hop(half, 6))
    with jax.named_scope("share_pair"):
        other = hop(half, 1)
    scale = 1.0 / math.sqrt(data_count * cam_count * pixels)
    return adam_update(core, half, other, w_head, master, first_moment, second_moment, scale)


def solution(mesh):
    placed = (
        P("dp", "cam", None),
        P("dp", "cam", None),
        P(),
        P("dp", "cam", None),
        P("dp", "cam", None, None),
        P("dp", "cam", None),
        P("dp", None),
        P("dp", None),
        P("dp", None),
    )
    return jax.shard_map(
        shards,
        mesh=mesh,
        in_specs=placed,
        out_specs=(P("dp", None), P("dp", None), P("dp", None)),
        check_vma=False,
    )
```

```python
import functools
import math

import jax
import jax.numpy as jnp
from jax import lax
from jax.experimental import pallas as pl
from jax.experimental.pallas import tpu as pltpu
from jax.sharding import PartitionSpec as P

beta_one = 0.9
beta_two = 0.999
bias_one = 0.9999734386011124
bias_two = 0.0952078528862911
learn_rate = 0.01
adam_epsilon = 1e-08

bf16 = jnp.bfloat16
f32 = jnp.float32
i32 = jnp.int32

NT = (((1,), (1,)), ((), ()))
TN = (((0,), (0,)), ((), ()))

CHIPS = 4
CAP = 512
CH = 128
SUMS = 128
MIB = 1 << 20


def vmem():
    return pl.BlockSpec(memory_space=pltpu.VMEM)


def smem():
    return pl.BlockSpec(memory_space=pltpu.SMEM)


def split(value):
    high = value.astype(bf16)
    return high, (value - high.astype(f32)).astype(bf16)


def gather_kernel(me_ref, lists_ref, tile_ref, own_ref, pair_ref, one_ref, two_ref, three_ref, wide, rows):
    wide[...] = tile_ref[...].astype(f32)
    me = me_ref[0]
    places = (
        (own_ref, 0), (pair_ref, 0), (one_ref, 0), (one_ref, 1),
        (two_ref, 0), (two_ref, 1), (three_ref, 0), (three_ref, 1),
    )
    for block, (ref, part) in enumerate(places):
        start = jnp.bitwise_xor(me, block) * CAP

        def step(i, carry):
            base = i * 64
            for u in range(64):
                cell = lists_ref[start + base + u]
                rows[pl.ds(base + u, 1), :] = wide[pl.ds(cell, 1), :]
            return carry

        lax.fori_loop(0, CAP // 64, step, 0)
        ref[part] = rows[...].astype(bf16)


def gather_rows(me, lists, tile):
    one = jax.ShapeDtypeStruct((1, CAP, CH), bf16)
    two = jax.ShapeDtypeStruct((2, CAP, CH), bf16)
    return pl.pallas_call(
        gather_kernel,
        out_shape=(one, one, two, two, two),
        in_specs=[smem(), smem(), vmem()],
        out_specs=(vmem(),) * 5,
        scratch_shapes=[pltpu.VMEM(tile.shape, f32), pltpu.VMEM((CAP, CH), f32)],
        compiler_params=pltpu.CompilerParams(vmem_limit_bytes=16 * MIB),
        name="gather_rows",
    )(me, lists, tile)


def head_kernel(me_ref, feat_ref, w_ref, slot_ref, occ_ref, ctx_ref, place_ref):
    head = lax.dot_general(feat_ref[...], w_ref[...], NT, preferred_element_type=f32)
    ctx_ref[:, :CH], ctx_ref[:, CH:] = split(head[:, :CH])
    occ = 1.0 / (1.0 + jnp.exp(-head[:, CH:]))
    occ_ref[...] = jnp.concatenate([occ, occ], axis=1)
    slots = slot_ref[...].T
    tile = (slots >> 9) ^ me_ref[0]
    slots = jnp.where(slots < 8 * CAP, ((tile & 1) << 11) | ((tile >> 1) << 9) | (slots & (CAP - 1)), 8 * CAP)
    place_ref[...] = jnp.concatenate([slots, slots], axis=1)


def head_values(me, feat, w_head, slots, block=512):
    pixels, width = feat.shape

    def rows(height, lanes):
        return pl.BlockSpec((height, lanes), lambda i: (i, 0))

    return pl.pallas_call(
        head_kernel,
        grid=(pixels // block,),
        out_shape=(
            jax.ShapeDtypeStruct((pixels, 128), f32),
            jax.ShapeDtypeStruct((pixels, 2 * CH), bf16),
            jax.ShapeDtypeStruct((pixels, 128), i32),
        ),
        in_specs=[
            smem(),
            rows(block, width),
            pl.BlockSpec(w_head.shape, lambda i: (0, 0)),
            pl.BlockSpec((slots.shape[0], block), lambda i: (0, i)),
        ],
        out_specs=(rows(block, 128), rows(block, 2 * CH), rows(block, 128)),
        compiler_params=pltpu.CompilerParams(vmem_limit_bytes=60 * MIB),
        cost_estimate=pl.CostEstimate(flops=4 * 10**9, bytes_accessed=8 * 10**6, transcendentals=0),
        name="head_values",
    )(me, feat, w_head, slots)


def weights_kernel(*refs):
    occ_ref, place_ref, wts_ref, token_ref = refs[-4:]
    block = occ_ref.shape[0]
    token_ref[...] = jnp.zeros_like(token_ref)
    lane = lax.broadcasted_iota(i32, (1, 128), 1)
    lane16 = lax.broadcasted_iota(i32, (16, 128), 1)
    sub16 = lax.broadcasted_iota(i32, (16, 128), 0)
    half16 = (lane16 >= 64).astype(i32)
    masks = [((sub16 & 7) == 2 * j + half16).astype(f32).astype(bf16) for j in range(4)]
    low_rows = [(sub16 + 16 * t).astype(f32).astype(bf16) for t in range(16)]
    zero = jnp.zeros((16, 128), bf16)
    one = jnp.ones((16, 128), bf16)

    def build(i, carry):
        base = pl.multiple_of(i * 16, 16)
        pair = []
        for q in range(2):
            slot = place_ref[pl.ds(base + q * 8, 8), :]
            occ = occ_ref[pl.ds(base + q * 8, 8), :]
            high = (slot >> 8).astype(f32)
            low = (slot & 255).astype(f32)
            key = jnp.concatenate([high, high - 1.0], axis=0).astype(bf16)
            hits = [key == jnp.asarray(2.0 * t, bf16) for t in range(8)]
            occ_high, occ_low = split(jnp.concatenate([occ, occ], axis=0))
            left_high, left_low, right = [], [], []
            for j in range(4):
                part_high = occ_high * masks[j]
                part_low = occ_low * masks[j]
                left_high.append(jnp.concatenate([jnp.where(hit, part_high, zero) for hit in hits], axis=0))
                left_low.append(jnp.concatenate([jnp.where(hit, part_low, zero) for hit in hits], axis=0))
                row = jnp.where(lane < 64, low[2 * j : 2 * j + 1], low[2 * j + 1 : 2 * j + 2])
                row = jnp.broadcast_to(row, (16, 128)).astype(bf16)
                right.append(jnp.concatenate([jnp.where(rows == row, one, zero) for rows in low_rows], axis=0))
            left = jnp.concatenate(
                [jnp.concatenate(left_high, axis=1), jnp.concatenate(left_low, axis=1)], axis=0
            )
            both = lax.dot_general(left, jnp.concatenate(right, axis=1), NT, preferred_element_type=f32)
            pair.append(both[:128] + both[128:])
        for h in range(16):
            rows = slice(h * 8, h * 8 + 8)
            value = jnp.concatenate([pair[0][rows], pair[1][rows]], axis=0)
            columns = slice(h * 256, h * 256 + 256)
            wts_ref[pl.ds(base, 16), columns], wts_ref[pl.ds(block + base, 16), columns] = split(value)
        return carry

    lax.fori_loop(0, block // 16, build, 0, unroll=8)


def pixel_weights(after, occ, places, first, count, wts=None, block=SUMS):
    pixels = occ.shape[0]
    table = 8 * CAP
    operands = tuple(after) if wts is None else (wts, *after)
    return pl.pallas_call(
        weights_kernel,
        grid=(count,),
        out_shape=(jax.ShapeDtypeStruct((2 * pixels, table), bf16), jax.ShapeDtypeStruct((8, 128), f32)),
        in_specs=[pl.BlockSpec(memory_space=pl.ANY)] * len(operands)
        + [pl.BlockSpec((block, 128), lambda i: (i + first, 0))] * 2,
        out_specs=(
            pl.BlockSpec((2 * block, table), lambda i: (i + first, 0)),
            pl.BlockSpec((8, 128), lambda i: (0, 0)),
        ),
        input_output_aliases={} if wts is None else {0: 0},
        compiler_params=pltpu.CompilerParams(vmem_limit_bytes=50 * MIB),
        cost_estimate=pl.CostEstimate(flops=25 * 10**8 * count, bytes_accessed=3 * 10**6 * count, transcendentals=0),
        name="pixel_weights",
    )(*operands, occ, places)


def grads_kernel(
    core_ref, own_ref, one_ref, two_ref, three_ref, far_ref, wts_ref, occ_ref, place_ref, ctx_ref, x_hbm, feat_hbm,
    keep_ref, send_ref, table, flip, scores, mixed, picked, head, x_in, feat, sems, *, owners,
):
    step = pl.program_id(0)
    last = pl.num_programs(0) - 1
    block = occ_ref.shape[0]
    count = table.shape[0]
    chunks = count // 256
    x_copy = pltpu.make_async_copy(x_hbm, x_in, sems.at[0])
    feat_copy = pltpu.make_async_copy(feat_hbm, feat, sems.at[1])

    def score(i):
        columns = pl.ds(pl.multiple_of(i * 256, 256), 256)
        part = flip[:, columns]
        scores[step % 2, :, columns] = jnp.dot(
            ctx_ref[...], jnp.concatenate([part, part], axis=0), preferred_element_type=f32
        )

    def pick(i):
        old = (step + 1) % 2
        for q in range(block // chunks // 8):
            base = pl.multiple_of(i * (block // chunks), 8) + q * 8
            place = place_ref[pl.ds(base, 8), :]
            low = place & 127
            high = place >> 7
            total = jnp.zeros((8, 128), f32)
            for g in range(count // 128):
                found = jnp.take_along_axis(
                    scores[old, pl.ds(base, 8), g * 128 : (g + 1) * 128], low, axis=1, mode="promise_in_bounds"
                )
                total = jnp.where(high == g, found, total)
            picked[pl.ds(base, 8), :] = total

    def mix(i):
        rows = pl.ds(pl.multiple_of(i * 256, 256), 256)
        mixed[...] += jnp.dot(wts_ref[:, rows], table[rows, :], preferred_element_type=f32)

    def finish():
        rows = pl.ds(pl.multiple_of((step - 1) * block, block), block)
        occ = occ_ref[...]
        both = mixed[...].reshape(block // SUMS, 2, SUMS, CH)
        head[rows, :CH] = (both[:, 0] + both[:, 1]).reshape(block, CH).astype(bf16)
        head[rows, CH:] = (occ * (1.0 - occ) * picked[...]).astype(bf16)

    @pl.when(step == 0)
    def _():
        x_copy.start()
        feat_copy.start()
        for k, ref in enumerate((own_ref, one_ref, two_ref, three_ref)):
            table[k * CAP : (k + 1) * CAP, :] = ref[0]
        table[4 * CAP :, :] = far_ref[...]

        def body(i, carry):
            rows = pl.ds(pl.multiple_of(i * 256, 256), 256)
            flip[:, rows] = table[rows, :].T
            score(i)
            return carry

        lax.fori_loop(0, chunks, body, 0, unroll=8)

    @pl.when((step > 0) & (step < last))
    def _():
        mixed[...] = jnp.zeros_like(mixed)

        def body(i, carry):
            pick(i)
            score(i)
            mix(i)
            return carry

        lax.fori_loop(0, chunks, body, 0, unroll=8)
        finish()

    @pl.when(step == last)
    def _():
        mixed[...] = jnp.zeros_like(mixed)

        def body(i, carry):
            pick(i)
            mix(i)
            return carry

        lax.fori_loop(0, chunks, body, 0, unroll=8)
        finish()
        x_copy.wait()
        feat_copy.wait()
        rows, width = keep_ref.shape
        half_rows = rows // owners
        span = 384
        per_span = span // (2 * half_rows)
        grads = head[...]
        lane = lax.broadcasted_iota(i32, (1, 128), 1)
        first = core_ref[0] == 0
        for n in range(x_in.shape[1] // span):
            columns = slice(n * span, (n + 1) * span)
            left = lax.dot_general(x_in[:, columns], grads, TN, preferred_element_type=f32)
            right = lax.dot_general(feat[:, columns], grads, TN, preferred_element_type=f32)
            tail = jnp.where(lane < 64, left[:, CH:], right[:, CH:])
            full = jnp.concatenate([left[:, :CH], right[:, :CH], tail], axis=1)
            full = full.reshape(per_span, 2, half_rows, width)
            height = per_span * half_rows
            part = slice(n * height, (n + 1) * height)
            keep_ref[part] = jnp.where(first, full[:, 0], full[:, 1]).reshape(height, width)
            send_ref[part] = jnp.where(first, full[:, 1], full[:, 0]).reshape(height, width).astype(bf16)


def inner_halves(core, tables, wts, occ, places, ctx, x_in, feat, owners, block=256):
    pixels, width = feat.shape
    count = 8 * CAP
    blocks = pixels // block
    first = pl.BlockSpec((1, CAP, CH), lambda i: (0, 0, 0))
    half = (width // 2, 384)

    def behind(i):
        return (jnp.maximum(i - 1, 0), 0)

    return pl.pallas_call(
        functools.partial(grads_kernel, owners=owners),
        grid=(blocks + 1,),
        out_shape=(jax.ShapeDtypeStruct(half, f32), jax.ShapeDtypeStruct(half, bf16)),
        in_specs=[
            smem(),
            first, first, first, first,
            pl.BlockSpec((4 * CAP, CH), lambda i: (0, 0)),
            pl.BlockSpec((2 * block, count), behind),
            pl.BlockSpec((block, 128), behind),
            pl.BlockSpec((block, 128), behind),
            pl.BlockSpec((block, 2 * CH), lambda i: (jnp.minimum(i, blocks - 1), 0)),
            pl.BlockSpec(memory_space=pl.ANY),
            pl.BlockSpec(memory_space=pl.ANY),
        ],
        out_specs=(vmem(), vmem()),
        scratch_shapes=[
            pltpu.VMEM((count, CH), bf16),
            pltpu.VMEM((CH, count), bf16),
            pltpu.VMEM((2, block, count), f32),
            pltpu.VMEM((2 * block, CH), f32),
            pltpu.VMEM((block, 128), f32),
            pltpu.VMEM((pixels, 256), bf16),
            pltpu.VMEM((pixels, width), bf16),
            pltpu.VMEM((pixels, width), bf16),
            pltpu.SemaphoreType.DMA((2,)),
        ],
        compiler_params=pltpu.CompilerParams(vmem_limit_bytes=50 * MIB),
        name="inner_halves",
    )(core, *tables, wts, occ, places, ctx, x_in, feat)


def adam_kernel(core_ref, mine_ref, other_ref, w_ref, master_ref, first_ref, second_ref, out_m, out_f, out_s, *, scale):
    mine, other = mine_ref[...], other_ref[...]
    upper = core_ref[0] == 0
    inner = jnp.concatenate([jnp.where(upper, mine, other), jnp.where(upper, other, mine)], axis=0)
    rows = inner.shape[0]
    proj = jnp.concatenate([inner[:, :CH], inner[:, 2 * CH : 2 * CH + 64]], axis=1)
    high = proj.astype(bf16)
    rest = proj - high.astype(f32)
    mid, low = split(rest)
    three = jnp.dot(jnp.concatenate([high, mid, low], axis=0), w_ref[...], preferred_element_type=f32)
    wide = three[2 * rows :] + three[rows : 2 * rows] + three[:rows]
    tail = jnp.concatenate([inner[:, CH : 2 * CH], inner[:, 2 * CH + 64 :]], axis=1)
    gradient = jnp.concatenate([wide, tail], axis=1) * scale
    first_new = beta_one * first_ref[...] + (1.0 - beta_one) * gradient
    second_new = beta_two * second_ref[...] + (1.0 - beta_two) * gradient * gradient
    direction = first_new / bias_one / (jnp.sqrt(second_new / bias_two) + adam_epsilon)
    out_m[...] = master_ref[...] - learn_rate * direction
    out_f[...] = first_new
    out_s[...] = second_new


def adam_update(core, mine, other, w_head, master, first, second, scale):
    out = jax.ShapeDtypeStruct(master.shape, f32)
    return pl.pallas_call(
        functools.partial(adam_kernel, scale=scale),
        out_shape=(out, out, out),
        in_specs=[smem()] + [vmem()] * 6,
        out_specs=(vmem(),) * 3,
        compiler_params=pltpu.CompilerParams(vmem_limit_bytes=32 * MIB),
        name="adam_update",
    )(core, mine, other, w_head, master, first, second)


def hop(value, distance):
    return lax.ppermute(value, "cam", [(i, i ^ distance) for i in range(2 * CHIPS)])


def shards(x_in, feat, w_head, g_bev, cell_lists, point_slots, master, first_moment, second_moment):
    cam_count = lax.axis_size("cam")
    data_count = lax.axis_size("dp")
    me = lax.axis_index("cam").astype(i32)
    core = (me & 1).reshape(1)
    features = feat[0]
    pixels = features.shape[0]
    w_head = w_head.T

    with jax.named_scope("lists"):
        lists = lax.all_to_all(cell_lists[0, 0], "cam", 0, 0, tiled=True)
    occ, ctx, places = head_values(me.reshape(1), features, w_head, point_slots[0].T)
    own, pair, one, two, three = gather_rows(me.reshape(1), lists.reshape(-1), g_bev[0])
    with jax.named_scope("rows"):
        one, two, three = hop(one, 2), hop(two, 4), hop(three, 6)
    wts, token = pixel_weights((own,), occ, places, 0, pixels // SUMS - 1)
    with jax.named_scope("rows_pair"):
        one, two, three, token = lax.optimization_barrier((one, two, three, token))
        far = hop(jnp.concatenate([pair[0], one[1], two[1], three[1]], axis=0), 1)
    wts, _ = pixel_weights((token,), occ, places, pixels // SUMS - 1, 1, wts)
    keep, send = inner_halves(
        core, (own, one, two, three, far), wts, occ, places, ctx, x_in[0], features, data_count
    )
    with jax.named_scope("sum_pair"):
        half = (keep + hop(send, 1).astype(f32)).astype(bf16)
        half = half.reshape(data_count, -1, half.shape[1])
    with jax.named_scope("sum_dp"):
        half = lax.all_to_all(half, "dp", 0, 0, tiled=True)
        half = jnp.sum(half.astype(f32), axis=0)
    with jax.named_scope("sum_x"):
        half = (half + hop(half, 2)) + (hop(half, 4) + hop(half, 6))
    with jax.named_scope("share_pair"):
        other = hop(half, 1)
    scale = 1.0 / math.sqrt(data_count * cam_count * pixels)
    return adam_update(core, half, other, w_head, master, first_moment, second_moment, scale)


def solution(mesh):
    placed = (
        P("dp", "cam", None),
        P("dp", "cam", None),
        P(),
        P("dp", "cam", None),
        P("dp", "cam", None, None),
        P("dp", "cam", None),
        P("dp", None),
        P("dp", None),
        P("dp", None),
    )
    return jax.shard_map(
        shards,
        mesh=mesh,
        in_specs=placed,
        out_specs=(P("dp", None), P("dp", None), P("dp", None)),
        check_vma=False,
    )
```

```python
import functools
import math

import jax
import jax.numpy as jnp
from jax import lax
from jax.experimental import pallas as pl
from jax.experimental.pallas import tpu as pltpu
from jax.sharding import PartitionSpec as P

beta_one = 0.9
beta_two = 0.999
bias_one = 0.9999734386011124
bias_two = 0.0952078528862911
learn_rate = 0.01
adam_epsilon = 1e-08

bf16 = jnp.bfloat16
f32 = jnp.float32
i32 = jnp.int32

NT = (((1,), (1,)), ((), ()))
TN = (((0,), (0,)), ((), ()))

CHIPS = 4
CAP = 512
CH = 128
SUMS = 128
MIB = 1 << 20


def vmem():
    return pl.BlockSpec(memory_space=pltpu.VMEM)


def smem():
    return pl.BlockSpec(memory_space=pltpu.SMEM)


def split(value):
    high = value.astype(bf16)
    return high, (value - high.astype(f32)).astype(bf16)


def gather_kernel(me_ref, lists_ref, tile_ref, own_ref, pair_ref, one_ref, two_ref, three_ref, wide, rows):
    wide[...] = tile_ref[...].astype(f32)
    me = me_ref[0]
    places = (
        (own_ref, 0), (pair_ref, 0), (one_ref, 0), (one_ref, 1),
        (two_ref, 0), (two_ref, 1), (three_ref, 0), (three_ref, 1),
    )
    for block, (ref, part) in enumerate(places):
        start = jnp.bitwise_xor(me, block) * CAP

        def step(i, carry):
            base = i * 64
            for u in range(64):
                cell = lists_ref[start + base + u]
                rows[pl.ds(base + u, 1), :] = wide[pl.ds(cell, 1), :]
            return carry

        lax.fori_loop(0, CAP // 64, step, 0)
        ref[part] = rows[...].astype(bf16)


def gather_rows(me, lists, tile):
    one = jax.ShapeDtypeStruct((1, CAP, CH), bf16)
    two = jax.ShapeDtypeStruct((2, CAP, CH), bf16)
    return pl.pallas_call(
        gather_kernel,
        out_shape=(one, one, two, two, two),
        in_specs=[smem(), smem(), vmem()],
        out_specs=(vmem(),) * 5,
        scratch_shapes=[pltpu.VMEM(tile.shape, f32), pltpu.VMEM((CAP, CH), f32)],
        compiler_params=pltpu.CompilerParams(vmem_limit_bytes=16 * MIB),
        name="gather_rows",
    )(me, lists, tile)


def head_kernel(me_ref, feat_ref, w_ref, slot_ref, occ_ref, ctx_ref, place_ref):
    head = lax.dot_general(feat_ref[...], w_ref[...], NT, preferred_element_type=f32)
    ctx_ref[:, :CH], ctx_ref[:, CH:] = split(head[:, :CH])
    occ = 1.0 / (1.0 + jnp.exp(-head[:, CH:]))
    occ_ref[...] = jnp.concatenate([occ, occ], axis=1)
    slots = slot_ref[...].T
    tile = (slots >> 9) ^ me_ref[0]
    slots = jnp.where(slots < 8 * CAP, ((tile & 1) << 11) | ((tile >> 1) << 9) | (slots & (CAP - 1)), 8 * CAP)
    place_ref[...] = jnp.concatenate([slots, slots], axis=1)


def head_values(me, feat, w_head, slots, block=512):
    pixels, width = feat.shape

    def rows(height, lanes):
        return pl.BlockSpec((height, lanes), lambda i: (i, 0))

    return pl.pallas_call(
        head_kernel,
        grid=(pixels // block,),
        out_shape=(
            jax.ShapeDtypeStruct((pixels, 128), f32),
            jax.ShapeDtypeStruct((pixels, 2 * CH), bf16),
            jax.ShapeDtypeStruct((pixels, 128), i32),
        ),
        in_specs=[
            smem(),
            rows(block, width),
            pl.BlockSpec(w_head.shape, lambda i: (0, 0)),
            pl.BlockSpec((slots.shape[0], block), lambda i: (0, i)),
        ],
        out_specs=(rows(block, 128), rows(block, 2 * CH), rows(block, 128)),
        compiler_params=pltpu.CompilerParams(vmem_limit_bytes=60 * MIB),
        cost_estimate=pl.CostEstimate(flops=4 * 10**9, bytes_accessed=8 * 10**6, transcendentals=0),
        name="head_values",
    )(me, feat, w_head, slots)


def weights_kernel(*refs):
    occ_ref, place_ref, wts_ref, token_ref = refs[-4:]
    block = occ_ref.shape[0]
    token_ref[...] = jnp.zeros_like(token_ref)
    lane = lax.broadcasted_iota(i32, (1, 128), 1)
    lane16 = lax.broadcasted_iota(i32, (16, 128), 1)
    sub16 = lax.broadcasted_iota(i32, (16, 128), 0)
    half16 = (lane16 >= 64).astype(i32)
    masks = [((sub16 & 7) == 2 * j + half16).astype(f32).astype(bf16) for j in range(4)]
    low_rows = [(sub16 + 16 * t).astype(f32).astype(bf16) for t in range(16)]
    zero = jnp.zeros((16, 128), bf16)
    one = jnp.ones((16, 128), bf16)

    def build(i, carry):
        base = pl.multiple_of(i * 16, 16)
        pair = []
        for q in range(2):
            slot = place_ref[pl.ds(base + q * 8, 8), :]
            occ = occ_ref[pl.ds(base + q * 8, 8), :]
            high = (slot >> 8).astype(f32)
            low = (slot & 255).astype(f32)
            key = jnp.concatenate([high, high - 1.0], axis=0).astype(bf16)
            hits = [key == jnp.asarray(2.0 * t, bf16) for t in range(8)]
            occ_high, occ_low = split(jnp.concatenate([occ, occ], axis=0))
            left_high, left_low, right = [], [], []
            for j in range(4):
                part_high = occ_high * masks[j]
                part_low = occ_low * masks[j]
                left_high.append(jnp.concatenate([jnp.where(hit, part_high, zero) for hit in hits], axis=0))
                left_low.append(jnp.concatenate([jnp.where(hit, part_low, zero) for hit in hits], axis=0))
                row = jnp.where(lane < 64, low[2 * j : 2 * j + 1], low[2 * j + 1 : 2 * j + 2])
                row = jnp.broadcast_to(row, (16, 128)).astype(bf16)
                right.append(jnp.concatenate([jnp.where(rows == row, one, zero) for rows in low_rows], axis=0))
            left = jnp.concatenate(
                [jnp.concatenate(left_high, axis=1), jnp.concatenate(left_low, axis=1)], axis=0
            )
            both = lax.dot_general(left, jnp.concatenate(right, axis=1), NT, preferred_element_type=f32)
            pair.append(both[:128] + both[128:])
        for h in range(16):
            rows = slice(h * 8, h * 8 + 8)
            value = jnp.concatenate([pair[0][rows], pair[1][rows]], axis=0)
            columns = slice(h * 256, h * 256 + 256)
            wts_ref[pl.ds(base, 16), columns], wts_ref[pl.ds(block + base, 16), columns] = split(value)
        return carry

    lax.fori_loop(0, block // 16, build, 0, unroll=8)


def pixel_weights(after, occ, places, first, count, wts=None, block=SUMS):
    pixels = occ.shape[0]
    table = 8 * CAP
    operands = tuple(after) if wts is None else (wts, *after)
    return pl.pallas_call(
        weights_kernel,
        grid=(count,),
        out_shape=(jax.ShapeDtypeStruct((2 * pixels, table), bf16), jax.ShapeDtypeStruct((8, 128), f32)),
        in_specs=[pl.BlockSpec(memory_space=pl.ANY)] * len(operands)
        + [pl.BlockSpec((block, 128), lambda i: (i + first, 0))] * 2,
        out_specs=(
            pl.BlockSpec((2 * block, table), lambda i: (i + first, 0)),
            pl.BlockSpec((8, 128), lambda i: (0, 0)),
        ),
        input_output_aliases={} if wts is None else {0: 0},
        compiler_params=pltpu.CompilerParams(vmem_limit_bytes=50 * MIB),
        cost_estimate=pl.CostEstimate(flops=25 * 10**8 * count, bytes_accessed=3 * 10**6 * count, transcendentals=0),
        name="pixel_weights",
    )(*operands, occ, places)


def grads_kernel(
    core_ref, own_ref, one_ref, two_ref, three_ref, far_ref, wts_ref, occ_ref, place_ref, ctx_ref, x_hbm, feat_hbm,
    keep_ref, send_ref, table, flip, scores, mixed, picked, head, x_in, feat, sems, *, owners,
):
    step = pl.program_id(0)
    last = pl.num_programs(0) - 1
    block = occ_ref.shape[0]
    count = table.shape[0]
    chunks = count // 256
    x_copy = pltpu.make_async_copy(x_hbm, x_in, sems.at[0])
    feat_copy = pltpu.make_async_copy(feat_hbm, feat, sems.at[1])

    def score(i):
        columns = pl.ds(pl.multiple_of(i * 256, 256), 256)
        part = flip[:, columns]
        scores[step % 2, :, columns] = jnp.dot(
            ctx_ref[...], jnp.concatenate([part, part], axis=0), preferred_element_type=f32
        )

    def pick(i):
        old = (step + 1) % 2
        for q in range(block // chunks // 8):
            base = pl.multiple_of(i * (block // chunks), 8) + q * 8
            place = place_ref[pl.ds(base, 8), :]
            low = place & 127
            high = place >> 7
            total = jnp.zeros((8, 128), f32)
            for g in range(count // 128):
                found = jnp.take_along_axis(
                    scores[old, pl.ds(base, 8), g * 128 : (g + 1) * 128], low, axis=1, mode="promise_in_bounds"
                )
                total = jnp.where(high == g, found, total)
            picked[pl.ds(base, 8), :] = total

    def mix(i):
        rows = pl.ds(pl.multiple_of(i * 256, 256), 256)
        mixed[...] += jnp.dot(wts_ref[:, rows], table[rows, :], preferred_element_type=f32)

    def finish():
        rows = pl.ds(pl.multiple_of((step - 1) * block, block), block)
        occ = occ_ref[...]
        both = mixed[...].reshape(block // SUMS, 2, SUMS, CH)
        head[rows, :CH] = (both[:, 0] + both[:, 1]).reshape(block, CH).astype(bf16)
        head[rows, CH:] = (occ * (1.0 - occ) * picked[...]).astype(bf16)

    @pl.when(step == 0)
    def _():
        x_copy.start()
        feat_copy.start()
        for k, ref in enumerate((own_ref, one_ref, two_ref, three_ref)):
            table[k * CAP : (k + 1) * CAP, :] = ref[0]
        table[4 * CAP :, :] = far_ref[...]

        def body(i, carry):
            rows = pl.ds(pl.multiple_of(i * 256, 256), 256)
            flip[:, rows] = table[rows, :].T
            score(i)
            return carry

        lax.fori_loop(0, chunks, body, 0, unroll=8)

    @pl.when((step > 0) & (step < last))
    def _():
        mixed[...] = jnp.zeros_like(mixed)

        def body(i, carry):
            pick(i)
            score(i)
            mix(i)
            return carry

        lax.fori_loop(0, chunks, body, 0, unroll=8)
        finish()

    @pl.when(step == last)
    def _():
        mixed[...] = jnp.zeros_like(mixed)

        def body(i, carry):
            pick(i)
            mix(i)
            return carry

        lax.fori_loop(0, chunks, body, 0, unroll=8)
        finish()
        x_copy.wait()
        feat_copy.wait()
        rows, width = keep_ref.shape
        half_rows = rows // owners
        span = 384
        per_span = span // (2 * half_rows)
        grads = head[...]
        lane = lax.broadcasted_iota(i32, (1, 128), 1)
        first = core_ref[0] == 0
        for n in range(x_in.shape[1] // span):
            columns = slice(n * span, (n + 1) * span)
            left = lax.dot_general(x_in[:, columns], grads, TN, preferred_element_type=f32)
            right = lax.dot_general(feat[:, columns], grads, TN, preferred_element_type=f32)
            tail = jnp.where(lane < 64, left[:, CH:], right[:, CH:])
            full = jnp.concatenate([left[:, :CH], right[:, :CH], tail], axis=1)
            full = full.reshape(per_span, 2, half_rows, width)
            height = per_span * half_rows
            part = slice(n * height, (n + 1) * height)
            keep_ref[part] = jnp.where(first, full[:, 0], full[:, 1]).reshape(height, width)
            send_ref[part] = jnp.where(first, full[:, 1], full[:, 0]).reshape(height, width).astype(bf16)


def inner_halves(core, tables, wts, occ, places, ctx, x_in, feat, owners, block=256):
    pixels, width = feat.shape
    count = 8 * CAP
    blocks = pixels // block
    first = pl.BlockSpec((1, CAP, CH), lambda i: (0, 0, 0))
    half = (width // 2, 384)

    def behind(i):
        return (jnp.maximum(i - 1, 0), 0)

    return pl.pallas_call(
        functools.partial(grads_kernel, owners=owners),
        grid=(blocks + 1,),
        out_shape=(jax.ShapeDtypeStruct(half, f32), jax.ShapeDtypeStruct(half, bf16)),
        in_specs=[
            smem(),
            first, first, first, first,
            pl.BlockSpec((4 * CAP, CH), lambda i: (0, 0)),
            pl.BlockSpec((2 * block, count), behind),
            pl.BlockSpec((block, 128), behind),
            pl.BlockSpec((block, 128), behind),
            pl.BlockSpec((block, 2 * CH), lambda i: (jnp.minimum(i, blocks - 1), 0)),
            pl.BlockSpec(memory_space=pl.ANY),
            pl.BlockSpec(memory_space=pl.ANY),
        ],
        out_specs=(vmem(), vmem()),
        scratch_shapes=[
            pltpu.VMEM((count, CH), bf16),
            pltpu.VMEM((CH, count), bf16),
            pltpu.VMEM((2, block, count), f32),
            pltpu.VMEM((2 * block, CH), f32),
            pltpu.VMEM((block, 128), f32),
            pltpu.VMEM((pixels, 256), bf16),
            pltpu.VMEM((pixels, width), bf16),
            pltpu.VMEM((pixels, width), bf16),
            pltpu.SemaphoreType.DMA((2,)),
        ],
        compiler_params=pltpu.CompilerParams(vmem_limit_bytes=50 * MIB),
        name="inner_halves",
    )(core, *tables, wts, occ, places, ctx, x_in, feat)


def adam_kernel(core_ref, mine_ref, other_ref, w_ref, master_ref, first_ref, second_ref, out_m, out_f, out_s, *, scale):
    mine, other = mine_ref[...], other_ref[...]
    upper = core_ref[0] == 0
    inner = jnp.concatenate([jnp.where(upper, mine, other), jnp.where(upper, other, mine)], axis=0)
    rows = inner.shape[0]
    proj = jnp.concatenate([inner[:, :CH], inner[:, 2 * CH : 2 * CH + 64]], axis=1)
    high = proj.astype(bf16)
    rest = proj - high.astype(f32)
    mid, low = split(rest)
    three = jnp.dot(jnp.concatenate([high, mid, low], axis=0), w_ref[...], preferred_element_type=f32)
    wide = three[2 * rows :] + three[rows : 2 * rows] + three[:rows]
    tail = jnp.concatenate([inner[:, CH : 2 * CH], inner[:, 2 * CH + 64 :]], axis=1)
    gradient = jnp.concatenate([wide, tail], axis=1) * scale
    first_new = beta_one * first_ref[...] + (1.0 - beta_one) * gradient
    second_new = beta_two * second_ref[...] + (1.0 - beta_two) * gradient * gradient
    direction = first_new / bias_one / (jnp.sqrt(second_new / bias_two) + adam_epsilon)
    out_m[...] = master_ref[...] - learn_rate * direction
    out_f[...] = first_new
    out_s[...] = second_new


def adam_update(core, mine, other, w_head, master, first, second, scale):
    out = jax.ShapeDtypeStruct(master.shape, f32)
    return pl.pallas_call(
        functools.partial(adam_kernel, scale=scale),
        out_shape=(out, out, out),
        in_specs=[smem()] + [vmem()] * 6,
        out_specs=(vmem(),) * 3,
        compiler_params=pltpu.CompilerParams(vmem_limit_bytes=32 * MIB),
        name="adam_update",
    )(core, mine, other, w_head, master, first, second)


def hop(value, distance):
    return lax.ppermute(value, "cam", [(i, i ^ distance) for i in range(2 * CHIPS)])


def shards(x_in, feat, w_head, g_bev, cell_lists, point_slots, master, first_moment, second_moment):
    cam_count = lax.axis_size("cam")
    data_count = lax.axis_size("dp")
    me = lax.axis_index("cam").astype(i32)
    core = (me & 1).reshape(1)
    features = feat[0]
    pixels = features.shape[0]
    w_head = w_head.T

    with jax.named_scope("lists"):
        lists = lax.all_to_all(cell_lists[0, 0], "cam", 0, 0, tiled=True)
    occ, ctx, places = head_values(me.reshape(1), features, w_head, point_slots[0].T)
    own, pair, one, two, three = gather_rows(me.reshape(1), lists.reshape(-1), g_bev[0])
    with jax.named_scope("rows"):
        one, two, three = hop(one, 2), hop(two, 4), hop(three, 6)
    wts, token = pixel_weights((own,), occ, places, 0, pixels // SUMS - 1)
    with jax.named_scope("rows_pair"):
        one, two, three, token = lax.optimization_barrier((one, two, three, token))
        far = hop(jnp.concatenate([pair[0], one[1], two[1], three[1]], axis=0), 1)
    wts, _ = pixel_weights((token,), occ, places, pixels // SUMS - 1, 1, wts)
    keep, send = inner_halves(
        core, (own, one, two, three, far), wts, occ, places, ctx, x_in[0], features, data_count
    )
    with jax.named_scope("sum_pair"):
        half = (keep + hop(send, 1).astype(f32)).astype(bf16)
        half = half.reshape(data_count, -1, half.shape[1])
    with jax.named_scope("sum_dp"):
        half = lax.all_to_all(half, "dp", 0, 0, tiled=True)
        half = jnp.sum(half.astype(f32), axis=0)
    with jax.named_scope("sum_x"):
        half = half + hop(half, 2)
        half = half + hop(half, 6)
    with jax.named_scope("share_pair"):
        other = hop(half, 1)
    scale = 1.0 / math.sqrt(data_count * cam_count * pixels)
    return adam_update(core, half, other, w_head, master, first_moment, second_moment, scale)


def solution(mesh):
    placed = (
        P("dp", "cam", None),
        P("dp", "cam", None),
        P(),
        P("dp", "cam", None),
        P("dp", "cam", None, None),
        P("dp", "cam", None),
        P("dp", None),
        P("dp", None),
        P("dp", None),
    )
    return jax.shard_map(
        shards,
        mesh=mesh,
        in_specs=placed,
        out_specs=(P("dp", None), P("dp", None), P("dp", None)),
        check_vma=False,
    )
```

```python
import functools
import math

import jax
import jax.numpy as jnp
from jax import lax
from jax.experimental import pallas as pl
from jax.experimental.pallas import tpu as pltpu
from jax.sharding import PartitionSpec as P

beta_one = 0.9
beta_two = 0.999
bias_one = 0.9999734386011124
bias_two = 0.0952078528862911
learn_rate = 0.01
adam_epsilon = 1e-08

bf16 = jnp.bfloat16
f32 = jnp.float32
i32 = jnp.int32

NT = (((1,), (1,)), ((), ()))
TN = (((0,), (0,)), ((), ()))

CHIPS = 4
CAP = 512
CH = 128
SUMS = 128
MIB = 1 << 20


def vmem():
    return pl.BlockSpec(memory_space=pltpu.VMEM)


def smem():
    return pl.BlockSpec(memory_space=pltpu.SMEM)


def split(value):
    high = value.astype(bf16)
    return high, (value - high.astype(f32)).astype(bf16)


def gather_kernel(me_ref, lists_ref, tile_ref, own_ref, pair_ref, one_ref, two_ref, three_ref, wide, rows):
    wide[...] = tile_ref[...].astype(f32)
    me = me_ref[0]
    places = (
        (own_ref, 0), (pair_ref, 0), (one_ref, 0), (one_ref, 1),
        (two_ref, 0), (two_ref, 1), (three_ref, 0), (three_ref, 1),
    )
    for block, (ref, part) in enumerate(places):
        start = jnp.bitwise_xor(me, block) * CAP

        def step(i, carry):
            base = i * 64
            for u in range(64):
                cell = lists_ref[start + base + u]
                rows[pl.ds(base + u, 1), :] = wide[pl.ds(cell, 1), :]
            return carry

        lax.fori_loop(0, CAP // 64, step, 0)
        ref[part] = rows[...].astype(bf16)


def gather_rows(me, lists, tile):
    one = jax.ShapeDtypeStruct((1, CAP, CH), bf16)
    two = jax.ShapeDtypeStruct((2, CAP, CH), bf16)
    return pl.pallas_call(
        gather_kernel,
        out_shape=(one, one, two, two, two),
        in_specs=[smem(), smem(), vmem()],
        out_specs=(vmem(),) * 5,
        scratch_shapes=[pltpu.VMEM(tile.shape, f32), pltpu.VMEM((CAP, CH), f32)],
        compiler_params=pltpu.CompilerParams(vmem_limit_bytes=16 * MIB),
        name="gather_rows",
    )(me, lists, tile)


def head_kernel(me_ref, feat_ref, w_ref, slot_ref, occ_ref, ctx_ref, place_ref):
    head = lax.dot_general(feat_ref[...], w_ref[...], NT, preferred_element_type=f32)
    ctx_ref[:, :CH], ctx_ref[:, CH:] = split(head[:, :CH])
    occ = 1.0 / (1.0 + jnp.exp(-head[:, CH:]))
    occ_ref[...] = jnp.concatenate([occ, occ], axis=1)
    slots = slot_ref[...].T
    tile = (slots >> 9) ^ me_ref[0]
    slots = jnp.where(slots < 8 * CAP, ((tile & 1) << 11) | ((tile >> 1) << 9) | (slots & (CAP - 1)), 8 * CAP)
    place_ref[...] = jnp.concatenate([slots, slots], axis=1)


def head_values(me, feat, w_head, slots, block=512):
    pixels, width = feat.shape

    def rows(height, lanes):
        return pl.BlockSpec((height, lanes), lambda i: (i, 0))

    return pl.pallas_call(
        head_kernel,
        grid=(pixels // block,),
        out_shape=(
            jax.ShapeDtypeStruct((pixels, 128), f32),
            jax.ShapeDtypeStruct((pixels, 2 * CH), bf16),
            jax.ShapeDtypeStruct((pixels, 128), i32),
        ),
        in_specs=[
            smem(),
            rows(block, width),
            pl.BlockSpec(w_head.shape, lambda i: (0, 0)),
            pl.BlockSpec((slots.shape[0], block), lambda i: (0, i)),
        ],
        out_specs=(rows(block, 128), rows(block, 2 * CH), rows(block, 128)),
        compiler_params=pltpu.CompilerParams(vmem_limit_bytes=52 * MIB),
        cost_estimate=pl.CostEstimate(flops=4 * 10**9, bytes_accessed=8 * 10**6, transcendentals=0),
        name="head_values",
    )(me, feat, w_head, slots)


def weights_kernel(*refs):
    occ_ref, place_ref, wts_ref, token_ref = refs[-4:]
    block = occ_ref.shape[0]
    token_ref[...] = jnp.zeros_like(token_ref)
    lane = lax.broadcasted_iota(i32, (1, 128), 1)
    lane16 = lax.broadcasted_iota(i32, (16, 128), 1)
    sub16 = lax.broadcasted_iota(i32, (16, 128), 0)
    half16 = (lane16 >= 64).astype(i32)
    masks = [((sub16 & 7) == 2 * j + half16).astype(f32).astype(bf16) for j in range(4)]
    low_rows = [(sub16 + 16 * t).astype(f32).astype(bf16) for t in range(16)]
    zero = jnp.zeros((16, 128), bf16)
    one = jnp.ones((16, 128), bf16)

    def build(i, carry):
        base = pl.multiple_of(i * 16, 16)
        pair = []
        for q in range(2):
            slot = place_ref[pl.ds(base + q * 8, 8), :]
            occ = occ_ref[pl.ds(base + q * 8, 8), :]
            high = (slot >> 8).astype(f32)
            low = (slot & 255).astype(f32)
            key = jnp.concatenate([high, high - 1.0], axis=0).astype(bf16)
            hits = [key == jnp.asarray(2.0 * t, bf16) for t in range(8)]
            occ_high, occ_low = split(jnp.concatenate([occ, occ], axis=0))
            left_high, left_low, right = [], [], []
            for j in range(4):
                part_high = occ_high * masks[j]
                part_low = occ_low * masks[j]
                left_high.append(jnp.concatenate([jnp.where(hit, part_high, zero) for hit in hits], axis=0))
                left_low.append(jnp.concatenate([jnp.where(hit, part_low, zero) for hit in hits], axis=0))
                row = jnp.where(lane < 64, low[2 * j : 2 * j + 1], low[2 * j + 1 : 2 * j + 2])
                row = jnp.broadcast_to(row, (16, 128)).astype(bf16)
                right.append(jnp.concatenate([jnp.where(rows == row, one, zero) for rows in low_rows], axis=0))
            left = jnp.concatenate(
                [jnp.concatenate(left_high, axis=1), jnp.concatenate(left_low, axis=1)], axis=0
            )
            both = lax.dot_general(left, jnp.concatenate(right, axis=1), NT, preferred_element_type=f32)
            pair.append(both[:128] + both[128:])
        for h in range(16):
            rows = slice(h * 8, h * 8 + 8)
            value = jnp.concatenate([pair[0][rows], pair[1][rows]], axis=0)
            columns = slice(h * 256, h * 256 + 256)
            wts_ref[pl.ds(base, 16), columns], wts_ref[pl.ds(block + base, 16), columns] = split(value)
        return carry

    lax.fori_loop(0, block // 16, build, 0, unroll=8)


def pixel_weights(after, occ, places, first, count, wts=None, block=SUMS):
    pixels = occ.shape[0]
    table = 8 * CAP
    operands = tuple(after) if wts is None else (wts, *after)
    return pl.pallas_call(
        weights_kernel,
        grid=(count,),
        out_shape=(jax.ShapeDtypeStruct((2 * pixels, table), bf16), jax.ShapeDtypeStruct((8, 128), f32)),
        in_specs=[pl.BlockSpec(memory_space=pl.ANY)] * len(operands)
        + [pl.BlockSpec((block, 128), lambda i: (i + first, 0))] * 2,
        out_specs=(
            pl.BlockSpec((2 * block, table), lambda i: (i + first, 0)),
            pl.BlockSpec((8, 128), lambda i: (0, 0)),
        ),
        input_output_aliases={} if wts is None else {0: 0},
        compiler_params=pltpu.CompilerParams(vmem_limit_bytes=50 * MIB),
        cost_estimate=pl.CostEstimate(flops=25 * 10**8 * count, bytes_accessed=3 * 10**6 * count, transcendentals=0),
        name="pixel_weights",
    )(*operands, occ, places)


def grads_kernel(
    core_ref, own_ref, one_ref, two_ref, three_ref, far_ref, wts_ref, occ_ref, place_ref, ctx_ref, x_hbm, feat_hbm,
    keep_ref, send_ref, table, flip, scores, mixed, picked, head, x_in, feat, sems, *, owners,
):
    step = pl.program_id(0)
    last = pl.num_programs(0) - 1
    block = occ_ref.shape[0]
    count = table.shape[0]
    chunks = count // 256
    x_copy = pltpu.make_async_copy(x_hbm, x_in, sems.at[0])
    feat_copy = pltpu.make_async_copy(feat_hbm, feat, sems.at[1])

    def score(i):
        columns = pl.ds(pl.multiple_of(i * 256, 256), 256)
        part = flip[:, columns]
        scores[step % 2, :, columns] = jnp.dot(
            ctx_ref[...], jnp.concatenate([part, part], axis=0), preferred_element_type=f32
        )

    def pick(i):
        old = (step + 1) % 2
        for q in range(block // chunks // 8):
            base = pl.multiple_of(i * (block // chunks), 8) + q * 8
            place = place_ref[pl.ds(base, 8), :]
            low = place & 127
            high = place >> 7
            total = jnp.zeros((8, 128), f32)
            for g in range(count // 128):
                found = jnp.take_along_axis(
                    scores[old, pl.ds(base, 8), g * 128 : (g + 1) * 128], low, axis=1, mode="promise_in_bounds"
                )
                total = jnp.where(high == g, found, total)
            picked[pl.ds(base, 8), :] = total

    def mix(i):
        rows = pl.ds(pl.multiple_of(i * 256, 256), 256)
        mixed[...] += jnp.dot(wts_ref[:, rows], table[rows, :], preferred_element_type=f32)

    def finish():
        rows = pl.ds(pl.multiple_of((step - 1) * block, block), block)
        occ = occ_ref[...]
        both = mixed[...].reshape(block // SUMS, 2, SUMS, CH)
        head[rows, :CH] = (both[:, 0] + both[:, 1]).reshape(block, CH).astype(bf16)
        head[rows, CH:] = (occ * (1.0 - occ) * picked[...]).astype(bf16)

    @pl.when(step == 0)
    def _():
        x_copy.start()
        feat_copy.start()
        for k, ref in enumerate((own_ref, one_ref, two_ref, three_ref)):
            table[k * CAP : (k + 1) * CAP, :] = ref[0]
        table[4 * CAP :, :] = far_ref[...]

        def body(i, carry):
            rows = pl.ds(pl.multiple_of(i * 256, 256), 256)
            flip[:, rows] = table[rows, :].T
            score(i)
            return carry

        lax.fori_loop(0, chunks, body, 0, unroll=8)

    @pl.when((step > 0) & (step < last))
    def _():
        mixed[...] = jnp.zeros_like(mixed)

        def body(i, carry):
            pick(i)
            score(i)
            mix(i)
            return carry

        lax.fori_loop(0, chunks, body, 0, unroll=8)
        finish()

    @pl.when(step == last)
    def _():
        mixed[...] = jnp.zeros_like(mixed)

        def body(i, carry):
            pick(i)
            mix(i)
            return carry

        lax.fori_loop(0, chunks, body, 0, unroll=8)
        finish()
        x_copy.wait()
        feat_copy.wait()
        rows, width = keep_ref.shape
        half_rows = rows // owners
        span = 384
        per_span = span // (2 * half_rows)
        grads = head[...]
        lane = lax.broadcasted_iota(i32, (1, 128), 1)
        first = core_ref[0] == 0
        for n in range(x_in.shape[1] // span):
            columns = slice(n * span, (n + 1) * span)
            left = lax.dot_general(x_in[:, columns], grads, TN, preferred_element_type=f32)
            right = lax.dot_general(feat[:, columns], grads, TN, preferred_element_type=f32)
            tail = jnp.where(lane < 64, left[:, CH:], right[:, CH:])
            full = jnp.concatenate([left[:, :CH], right[:, :CH], tail], axis=1)
            full = full.reshape(per_span, 2, half_rows, width)
            height = per_span * half_rows
            part = slice(n * height, (n + 1) * height)
            keep_ref[part] = jnp.where(first, full[:, 0], full[:, 1]).reshape(height, width)
            send_ref[part] = jnp.where(first, full[:, 1], full[:, 0]).reshape(height, width).astype(bf16)


def inner_halves(core, tables, wts, occ, places, ctx, x_in, feat, owners, block=256):
    pixels, width = feat.shape
    count = 8 * CAP
    blocks = pixels // block
    first = pl.BlockSpec((1, CAP, CH), lambda i: (0, 0, 0))
    half = (width // 2, 384)

    def behind(i):
        return (jnp.maximum(i - 1, 0), 0)

    return pl.pallas_call(
        functools.partial(grads_kernel, owners=owners),
        grid=(blocks + 1,),
        out_shape=(jax.ShapeDtypeStruct(half, f32), jax.ShapeDtypeStruct(half, bf16)),
        in_specs=[
            smem(),
            first, first, first, first,
            pl.BlockSpec((4 * CAP, CH), lambda i: (0, 0)),
            pl.BlockSpec((2 * block, count), behind),
            pl.BlockSpec((block, 128), behind),
            pl.BlockSpec((block, 128), behind),
            pl.BlockSpec((block, 2 * CH), lambda i: (jnp.minimum(i, blocks - 1), 0)),
            pl.BlockSpec(memory_space=pl.ANY),
            pl.BlockSpec(memory_space=pl.ANY),
        ],
        out_specs=(vmem(), vmem()),
        scratch_shapes=[
            pltpu.VMEM((count, CH), bf16),
            pltpu.VMEM((CH, count), bf16),
            pltpu.VMEM((2, block, count), f32),
            pltpu.VMEM((2 * block, CH), f32),
            pltpu.VMEM((block, 128), f32),
            pltpu.VMEM((pixels, 256), bf16),
            pltpu.VMEM((pixels, width), bf16),
            pltpu.VMEM((pixels, width), bf16),
            pltpu.SemaphoreType.DMA((2,)),
        ],
        compiler_params=pltpu.CompilerParams(vmem_limit_bytes=50 * MIB),
        name="inner_halves",
    )(core, *tables, wts, occ, places, ctx, x_in, feat)


def adam_kernel(core_ref, mine_ref, other_ref, w_ref, master_ref, first_ref, second_ref, out_m, out_f, out_s, *, scale):
    mine, other = mine_ref[...], other_ref[...]
    upper = core_ref[0] == 0
    inner = jnp.concatenate([jnp.where(upper, mine, other), jnp.where(upper, other, mine)], axis=0)
    rows = inner.shape[0]
    proj = jnp.concatenate([inner[:, :CH], inner[:, 2 * CH : 2 * CH + 64]], axis=1)
    high = proj.astype(bf16)
    rest = proj - high.astype(f32)
    mid, low = split(rest)
    three = jnp.dot(jnp.concatenate([high, mid, low], axis=0), w_ref[...], preferred_element_type=f32)
    wide = three[2 * rows :] + three[rows : 2 * rows] + three[:rows]
    tail = jnp.concatenate([inner[:, CH : 2 * CH], inner[:, 2 * CH + 64 :]], axis=1)
    gradient = jnp.concatenate([wide, tail], axis=1) * scale
    first_new = beta_one * first_ref[...] + (1.0 - beta_one) * gradient
    second_new = beta_two * second_ref[...] + (1.0 - beta_two) * gradient * gradient
    direction = first_new / bias_one / (jnp.sqrt(second_new / bias_two) + adam_epsilon)
    out_m[...] = master_ref[...] - learn_rate * direction
    out_f[...] = first_new
    out_s[...] = second_new


def adam_update(core, mine, other, w_head, master, first, second, scale):
    out = jax.ShapeDtypeStruct(master.shape, f32)
    return pl.pallas_call(
        functools.partial(adam_kernel, scale=scale),
        out_shape=(out, out, out),
        in_specs=[smem()] + [vmem()] * 6,
        out_specs=(vmem(),) * 3,
        compiler_params=pltpu.CompilerParams(vmem_limit_bytes=32 * MIB),
        name="adam_update",
    )(core, mine, other, w_head, master, first, second)


def hop(value, distance):
    return lax.ppermute(value, "cam", [(i, i ^ distance) for i in range(2 * CHIPS)])


def shards(x_in, feat, w_head, g_bev, cell_lists, point_slots, master, first_moment, second_moment):
    cam_count = lax.axis_size("cam")
    data_count = lax.axis_size("dp")
    me = lax.axis_index("cam").astype(i32)
    core = (me & 1).reshape(1)
    features = feat[0]
    pixels = features.shape[0]
    w_head = w_head.T

    with jax.named_scope("lists"):
        lists = lax.all_to_all(cell_lists[0, 0], "cam", 0, 0, tiled=True)
    occ, ctx, places = head_values(me.reshape(1), features, w_head, point_slots[0].T)
    own, pair, one, two, three = gather_rows(me.reshape(1), lists.reshape(-1), g_bev[0])
    with jax.named_scope("rows"):
        one, two, three = hop(one, 2), hop(two, 4), hop(three, 6)
    wts, token = pixel_weights((own,), occ, places, 0, pixels // SUMS - 1)
    with jax.named_scope("rows_pair"):
        one, two, three, token = lax.optimization_barrier((one, two, three, token))
        far = hop(jnp.concatenate([pair[0], one[1], two[1], three[1]], axis=0), 1)
    wts, _ = pixel_weights((token,), occ, places, pixels // SUMS - 1, 1, wts)
    keep, send = inner_halves(
        core, (own, one, two, three, far), wts, occ, places, ctx, x_in[0], features, data_count
    )
    with jax.named_scope("sum_pair"):
        half = (keep + hop(send, 1).astype(f32)).astype(bf16)
        half = half.reshape(data_count, -1, half.shape[1])
    with jax.named_scope("sum_dp"):
        half = lax.all_to_all(half, "dp", 0, 0, tiled=True)
        half = jnp.sum(half.astype(f32), axis=0)
    with jax.named_scope("sum_x"):
        half = (half + hop(half, 2)) + (hop(half, 4) + hop(half, 6))
    with jax.named_scope("share_pair"):
        other = hop(half, 1)
    scale = 1.0 / math.sqrt(data_count * cam_count * pixels)
    return adam_update(core, half, other, w_head, master, first_moment, second_moment, scale)


def solution(mesh):
    placed = (
        P("dp", "cam", None),
        P("dp", "cam", None),
        P(),
        P("dp", "cam", None),
        P("dp", "cam", None, None),
        P("dp", "cam", None),
        P("dp", None),
        P("dp", None),
        P("dp", None),
    )
    return jax.shard_map(
        shards,
        mesh=mesh,
        in_specs=placed,
        out_specs=(P("dp", None), P("dp", None), P("dp", None)),
        check_vma=False,
    )
```
